256 devices in a mesh: row: 16 (over x, y), col: 16 (over z, core).
Axes of the slice: x: 4, y: 4, z: 8, core: 2. Of those that a mesh axis runs over, the one named last changes fastest.
Arguments:
- incident: bfloat16 [65536, 256], P(('col', 'row')), may hold values from -6 to 6
- perm: int32 [512, 128], P(('col', 'row')), may hold values from 0 to 127, as said below
- far_u: bfloat16 [8192, 2, 128, 64], P(('row', 'col')), may hold values from -0.09375 to 0.09375
- far_v: bfloat16 [8192, 2, 128, 64], P(('row', 'col')), may hold values from -0.375 to 0.375
- far_rank: int32 [8192], P(('row', 'col')), may hold values from 16 to 64, as said below
- far_rows: int32 [8192], P(('row', 'col')), may hold values from 0 to 511, as said below
- far_cols: int32 [8192], P(('row', 'col')), may hold values from 0 to 511, as said below
- near_block: bfloat16 [7168, 2, 128, 128], P(('row', 'col')), may hold values from -0.0625 to 0.0625
- near_rows: int32 [7168], P(('row', 'col')), may hold values from 0 to 511, as said below
- near_cols: int32 [7168], P(('row', 'col')), may hold values from 0 to 511, as said below
Outputs:
- scattered: bfloat16 [65536, 256], P(('row', 'col'))
The draws below stay inside these ranges and needn't reach their ends.
Inputs may be any that keep to these rules, and one draw needn't show every extreme that they name: `perm`: each row is a permutation of 0 to 127. `far_rank`: each value is 16, 32 or 64. `far_rows`: block g lies on mesh device d = g // 32 (row index d // number of col devices, col index d % number of col devices); its row cluster lies among the 2 * (col devices) clusters of that row index's slab of the output. `far_cols`: block g lies on device d = g // 32; its column cluster lies among the 2 * (row devices) clusters that the devices of its col index hold of incident. `near_rows`: as for far_rows, with 28 blocks a device. `near_cols`: as for far_cols, with 28 blocks a device.
All inputs are finite; a program needn't handle non-finite values.
Results may differ from the reference program's by a relative error of at most 0.0035.
Values may be sent and summed in bfloat16 or wider, within the bound.
No kernel may reach another device: no remote copies, remote signals or barrier semaphores. Data moves between devices by JAX's collectives and lax.ppermute only.
A program may use at most 64 MiB of HBM per device.

```python
import jax
import jax.numpy as jnp
from jax import lax

LEAF = 128
RMAX = 64
CL_DEV = 2
NB_DEV = 32
NN_DEV = 28
COLS = 256
NC = 512
NTOT = 65536
NB_ALL = 8192
NN_ALL = 7168
N_ROW = 16
N_COL = 16
DEVICES = 256


def owner_slab(count, along_row):
    device = jnp.arange(count * DEVICES, dtype=jnp.int32) // count
    if along_row:
        return (device // N_COL * (CL_DEV * N_COL), CL_DEV * N_COL)
    return (device % N_COL * (CL_DEV * N_ROW), CL_DEV * N_ROW)


def cluster_draw(key, count, along_row):
    base, span = owner_slab(count, along_row)
    return base + jax.random.randint(key, base.shape, 0, span, dtype=jnp.int32)


def draw_perm(key, part):
    key = jax.random.fold_in(key, 17)
    keys = jax.random.split(key, NC)
    return jax.vmap(lambda single: jax.random.permutation(single, LEAF))(keys).astype(jnp.int32)


def draw_far_rank(key, part):
    key = jax.random.fold_in(key, 13)
    level = jax.random.randint(key, (NB_ALL,), 0, 3, dtype=jnp.int32)
    factor = jnp.where(level == 0, 1, jnp.where(level == 1, 2, 4)).astype(jnp.int32)
    return RMAX // 4 * factor


def draw_far_rows(key, part):
    key = jax.random.fold_in(key, 11)
    return cluster_draw(key, NB_DEV, True)


def draw_far_cols(key, part):
    key = jax.random.fold_in(key, 19)
    return cluster_draw(key, NB_DEV, False)


def draw_near_rows(key, part):
    key = jax.random.fold_in(key, 23)
    return cluster_draw(key, NN_DEV, True)


def draw_near_cols(key, part):
    key = jax.random.fold_in(key, 29)
    return cluster_draw(key, NN_DEV, False)


def levels(stream_key, shape, pieces, smallest, largest):
    loudness, own = 1.0, jax.random.fold_in(stream_key, 6)
    for position, parts in pieces:
        heights = jnp.exp(jax.random.uniform(jax.random.fold_in(own, position), (parts,), jnp.float32, smallest / len(pieces), largest / len(pieces)))
        loudness = loudness * jnp.repeat(heights, shape[position] // parts).reshape([-1 if axis == position else 1 for axis in range(len(shape))])
    return loudness


def bell_draw(rng, extent, scale, reach, shards=(), kind=jnp.bfloat16):
    factor_of = levels(rng, extent, shards, -0.22, 0.18) if shards else 1.0
    entries = jax.random.normal(rng, extent, jnp.float32) * scale * factor_of
    return jnp.minimum(jnp.maximum(entries, -reach), reach).astype(kind)


def setup_inputs(seed: int = 0) -> dict:
    streams_of = jax.random.split(jax.random.key(seed), 11)
    return {
        "incident": bell_draw(streams_of[0], (NTOT, COLS), 1.0, 6.0, ((0, 256),)),
        "perm": draw_perm(jax.random.fold_in(streams_of[10], 71), 0),
        "far_u": bell_draw(streams_of[2], (NB_ALL, 2, LEAF, RMAX), (4 * RMAX * NB_DEV // CL_DEV) ** -0.5, 0.09375, ((0, 256),)),
        "far_v": bell_draw(streams_of[3], (NB_ALL, 2, LEAF, RMAX), (2 * LEAF) ** -0.5, 0.375, ((0, 256),)),
        "far_rank": draw_far_rank(jax.random.fold_in(streams_of[10], 71), 0),
        "far_rows": draw_far_rows(jax.random.fold_in(streams_of[10], 71), 0),
        "far_cols": draw_far_cols(jax.random.fold_in(streams_of[10], 71), 0),
        "near_block": bell_draw(streams_of[7], (NN_ALL, 2, LEAF, LEAF), (4 * LEAF * NN_DEV // CL_DEV) ** -0.5, 0.0625, ((0, 256),)),
        "near_rows": draw_near_rows(jax.random.fold_in(streams_of[10], 71), 0),
        "near_cols": draw_near_cols(jax.random.fold_in(streams_of[10], 71), 0),
    }


def swap_parts(values):
    half = values.shape[-1] // 2
    return jnp.concatenate([-values[..., half:], values[..., :half]], axis=-1)


def product(form, left, right):
    return jnp.einsum(form, left, right, precision=lax.Precision.HIGHEST)


def reference(incident, perm, far_u, far_v, far_rank, far_rows, far_cols, near_block, near_rows, near_cols):
    width = incident.shape[1]
    ordered = jnp.take_along_axis(incident.reshape(NC, LEAF, width), perm.astype(jnp.int32)[:, :, None], axis=1)
    total = jnp.zeros((NC, LEAF, width), jnp.float32)

    def far_step(carry, group):
        upper, lower, rank, rows, cols = group
        trial = ordered[cols].astype(jnp.float32)
        lower = lower.astype(jnp.float32)
        upper = upper.astype(jnp.float32)
        coeff = product('blr,blc->brc', lower[:, 0], trial) + product('blr,blc->brc', lower[:, 1], swap_parts(trial))
        keep = (jnp.arange(RMAX, dtype=jnp.int32)[None, :] < rank[:, None]).astype(jnp.float32)
        coeff = lax.optimization_barrier((coeff * keep[:, :, None]).astype(jnp.bfloat16)).astype(jnp.float32)
        term = product('blr,brc->blc', upper[:, 0], coeff) + product('blr,brc->blc', upper[:, 1], swap_parts(coeff))
        return carry.at[rows].add(term), None

    def near_step(carry, group):
        block, rows, cols = group
        trial = ordered[cols].astype(jnp.float32)
        block = block.astype(jnp.float32)
        term = product('blm,bmc->blc', block[:, 0], trial) + product('blm,bmc->blc', block[:, 1], swap_parts(trial))
        return carry.at[rows].add(term), None

    far_groups = (far_u.reshape(DEVICES, NB_DEV, 2, LEAF, RMAX), far_v.reshape(DEVICES, NB_DEV, 2, LEAF, RMAX),
                  far_rank.reshape(DEVICES, NB_DEV), far_rows.reshape(DEVICES, NB_DEV), far_cols.reshape(DEVICES, NB_DEV))
    total, unused = lax.scan(far_step, total, far_groups)
    near_groups = (near_block.reshape(DEVICES, NN_DEV, 2, LEAF, LEAF), near_rows.reshape(DEVICES, NN_DEV),
                   near_cols.reshape(DEVICES, NN_DEV))
    total, unused = lax.scan(near_step, total, near_groups)
    return total.reshape(NTOT, width).astype(jnp.bfloat16)
```

```python
import jax
import jax.numpy as jnp
from jax import lax
from jax.experimental import pallas as pl
from jax.experimental.pallas import tpu as pltpu
from jax.sharding import PartitionSpec as P

LEAF = 128
COLS = 256
HALF = 128
RMAX = 64
NB = 32
NN = 28
NX = 4
NY = 4
NZ = 8
NCORE = 2
SLAB = 32
F32 = jnp.float32
BF16 = jnp.bfloat16
VMEM = pl.BlockSpec(memory_space=pltpu.VMEM)
SMEM = pl.BlockSpec(memory_space=pltpu.SMEM)


def row_pairs(dx, dy):
    return [
        (x * NY + y, (x + dx) % NX * NY + (y + dy) % NY) for x in range(NX) for y in range(NY)
    ]


def along_x(step, value):
    return lax.ppermute(value, "row", row_pairs(step, 0))


def along_y(step, value):
    return lax.ppermute(value, "row", row_pairs(0, step))


def swap_parts(values):
    return jnp.concatenate([-values[:, HALF:], values[:, :HALF]], axis=1)


def order_kernel(perm_ref, x_ref, even_ref, odd_ref):
    source = lax.broadcasted_iota(jnp.int32, (LEAF, LEAF), 0)
    for k, out in enumerate((even_ref, odd_ref)):
        chosen = (source == perm_ref[k : k + 1, :]).astype(F32).astype(BF16)
        out[...] = lax.dot_general(
            chosen,
            x_ref[k * LEAF : (k + 1) * LEAF, :],
            (((0,), (0,)), ((), ())),
            preferred_element_type=F32,
        ).astype(BF16)


def order(perm, incident):
    shape = jax.ShapeDtypeStruct((LEAF, COLS), BF16)
    return pl.pallas_call(
        order_kernel,
        out_shape=(shape, shape),
        in_specs=[VMEM, VMEM],
        out_specs=(VMEM, VMEM),
    )(perm, incident)


def prepare_kernel(rank_ref, u_ref, v_ref, u_out, v_out):
    line = lax.broadcasted_iota(jnp.int32, (RMAX, LEAF), 0)

    def step(b, carry):
        keep = line < rank_ref[b]
        for k in range(2):
            v = v_ref[b, k]
            v_out[b, :, k * LEAF : (k + 1) * LEAF] = jnp.where(keep, v.astype(F32), 0.0).astype(BF16)
        u_out[b] = jnp.concatenate([u_ref[b, 0], u_ref[b, 1]], axis=0).T
        return carry

    lax.fori_loop(0, NB, step, 0, unroll=4)


def prepare(rank, u, v):
    return pl.pallas_call(
        prepare_kernel,
        out_shape=(
            jax.ShapeDtypeStruct((NB, LEAF, 2 * RMAX), BF16),
            jax.ShapeDtypeStruct((NB, RMAX, 2 * LEAF), BF16),
        ),
        in_specs=[SMEM, VMEM, VMEM],
        out_specs=(VMEM, VMEM),
        cost_estimate=pl.CostEstimate(flops=0, bytes_accessed=8 << 20, transcendentals=0),
    )(rank, u, v)


def block_kernel(
    place_ref, far_rows, far_cols, near_rows, near_cols, *refs
):
    pieces = refs[:8]
    u_ref, v_ref, near_ref, other_ref, own_ref, trial, total = refs[8:]
    my_x, my_y, my_core = place_ref[0], place_ref[1], place_ref[2]

    def gray(d):
        return d ^ (d >> 1)

    def slot_of(cluster):
        k = cluster & (SLAB - 1)
        r = k >> 1
        dx = gray((my_x - (r >> 2)) & 3)
        dy = gray((my_y - (r & 3)) & 3)
        return jnp.where((k & 1) == 0, dy * 4 + dx, 16 + dx * 4 + dy)

    for p, piece in enumerate(pieces):
        for q in range(4):
            x = piece[q * LEAF : (q + 1) * LEAF, :]
            trial[p * 4 + q, :LEAF, :] = x
            trial[p * 4 + q, LEAF:, :] = swap_parts(x)
    total[...] = jnp.zeros_like(total)

    def add(row, term):
        total[row & (SLAB - 1)] += term

    def far_step(b, carry):
        x = trial[slot_of(far_cols[b])]
        coeff = jnp.dot(v_ref[b], x, preferred_element_type=F32).astype(BF16)
        both = jnp.concatenate([coeff, swap_parts(coeff)], axis=0)
        add(far_rows[b], jnp.dot(u_ref[b], both, preferred_element_type=F32))
        return carry

    def near_step(n, carry):
        x = trial[slot_of(near_cols[n])]
        block = jnp.concatenate([near_ref[n, 0], near_ref[n, 1]], axis=1)
        add(near_rows[n], jnp.dot(block, x, preferred_element_type=F32))
        return carry

    lax.fori_loop(0, NB, far_step, 0, unroll=4)
    lax.fori_loop(0, NN, near_step, 0, unroll=4)

    for z in range(NZ):
        for k in range(2):
            rows = slice((z * 2 + k) * LEAF, (z * 2 + k + 1) * LEAF)
            other_ref[rows, :] = total[z * 4 + (1 - my_core) * 2 + k].astype(BF16)
            own_ref[rows, :] = total[z * 4 + my_core * 2 + k]


def blocks(place, far_rows, far_cols, near_rows, near_cols, pieces, u, v, near):
    rows = NZ * 2 * LEAF
    return pl.pallas_call(
        block_kernel,
        out_shape=(
            jax.ShapeDtypeStruct((rows, COLS), BF16),
            jax.ShapeDtypeStruct((rows, COLS), F32),
        ),
        in_specs=[SMEM] * 5 + [VMEM] * 11,
        out_specs=(VMEM, VMEM),
        scratch_shapes=[
            pltpu.VMEM((SLAB, 2 * LEAF, COLS), BF16),
            pltpu.VMEM((SLAB, LEAF, COLS), F32),
        ],
        compiler_params=pltpu.CompilerParams(vmem_limit_bytes=40 << 20),
    )(place, far_rows, far_cols, near_rows, near_cols, *pieces, u, v, near)


def body(
    incident, perm, far_u, far_v, far_rank, far_rows, far_cols, near_block, near_rows, near_cols
):
    row, col = lax.axis_index("row"), lax.axis_index("col")
    place = jnp.stack([row // NY, row % NY, col % NCORE]).astype(jnp.int32)
    even, odd = order(perm, incident)
    u, v = prepare(far_rank, jnp.swapaxes(far_u, 2, 3), jnp.swapaxes(far_v, 2, 3))
    even_x = jnp.concatenate([even] + [along_x(s, even) for s in (1, -1, 2)], axis=0)
    odd_y = jnp.concatenate([odd] + [along_y(s, odd) for s in (1, -1, 2)], axis=0)
    pieces = [even_x] + [along_y(s, even_x) for s in (1, -1, 2)]
    pieces += [odd_y] + [along_x(s, odd_y) for s in (1, -1, 2)]
    other, own = blocks(
        place, far_rows, far_cols, near_rows, near_cols, pieces, u, v, near_block
    )
    swapped = lax.ppermute(other, "col", [(d, d ^ 1) for d in range(NZ * NCORE)])
    chip = (own + swapped.astype(F32)).astype(BF16)
    groups = [[z * NCORE + c for z in range(NZ)] for c in range(NCORE)]
    parts = lax.all_to_all(
        chip.reshape(NZ, 2 * LEAF, COLS), "col", 0, 0, tiled=True, axis_index_groups=groups
    )
    return jnp.sum(parts.astype(F32), axis=0).astype(BF16)


def solution(mesh):
    placed = (
        P(("col", "row"), None),
        P(("col", "row"), None),
        P(("row", "col"), None, None, None),
        P(("row", "col"), None, None, None),
        P(("row", "col")),
        P(("row", "col")),
        P(("row", "col")),
        P(("row", "col"), None, None, None),
        P(("row", "col")),
        P(("row", "col")),
    )
    return jax.shard_map(
        body, mesh=mesh, in_specs=placed, out_specs=P(("row", "col"), None), check_vma=False
    )
```

```python
import jax
import jax.numpy as jnp
from jax import lax
from jax.experimental import pallas as pl
from jax.experimental.pallas import tpu as pltpu
from jax.sharding import PartitionSpec as P

LEAF = 128
COLS = 256
HALF = 128
RMAX = 64
NB = 32
NN = 28
NX = 4
NY = 4
NZ = 8
NCORE = 2
SLAB = 32
WAYS = 4
STEPS = (4, 7, 1, 6, 2, 5, 3, 0)
F32 = jnp.float32
BF16 = jnp.bfloat16
VMEM = pl.BlockSpec(memory_space=pltpu.VMEM)
SMEM = pl.BlockSpec(memory_space=pltpu.SMEM)
ANY = pl.BlockSpec(memory_space=pl.ANY)


def limit(mib):
    return pltpu.CompilerParams(vmem_limit_bytes=mib << 20)


def position():
    row, col = lax.axis_index("row"), lax.axis_index("col")
    return row // NY, row % NY, col // NCORE, col % NCORE


def hop(turn, step, value):
    pairs = []
    for d in range(NX * NY * NZ * NCORE):
        row, col = divmod(d, NZ * NCORE)
        x, y = divmod(row, NY)
        if (col + turn) % NCORE == 0:
            x = (x + step) % NX
        else:
            y = (y + step) % NY
        pairs.append((d, (x * NY + y) * NZ * NCORE + col))
    return lax.ppermute(value, ("row", "col"), pairs)


def along_z(step, value):
    pairs = [
        (z * NCORE + c, (z + step) % NZ * NCORE + c) for z in range(NZ) for c in range(NCORE)
    ]
    return lax.ppermute(value, "col", pairs)


def other_core(value):
    return lax.ppermute(value, "col", [(d, d ^ 1) for d in range(NZ * NCORE)])


def after(value, earlier):
    return lax.optimization_barrier((value, earlier))[0]


def swap_parts(values):
    return jnp.concatenate([-values[:, HALF:], values[:, :HALF]], axis=1)


def order_kernel(perm_hbm, x_hbm, out_ref, perm_ref, x_ref, perm_sem, x_sem):
    x_copy = pltpu.make_async_copy(x_hbm, x_ref, x_sem)
    perm_copy = pltpu.make_async_copy(perm_hbm, perm_ref, perm_sem)
    x_copy.start()
    perm_copy.start()
    source = lax.broadcasted_iota(jnp.int32, (LEAF, LEAF), 0)
    perm_copy.wait()
    x_copy.wait()
    for k in range(2):
        rows = slice(k * LEAF, (k + 1) * LEAF)
        chosen = (source == perm_ref[k : k + 1, :]).astype(F32).astype(BF16)
        out_ref[rows, :] = lax.dot_general(
            chosen, x_ref[rows, :], (((0,), (0,)), ((), ())), preferred_element_type=F32
        ).astype(BF16)


def order(perm, incident):
    return pl.pallas_call(
        order_kernel,
        out_shape=pltpu.VMEM((2 * LEAF, COLS), BF16),
        in_specs=[ANY, ANY],
        out_specs=VMEM,
        scratch_shapes=[
            pltpu.VMEM((2, LEAF), jnp.int32),
            pltpu.VMEM((2 * LEAF, COLS), BF16),
            pltpu.SemaphoreType.DMA,
            pltpu.SemaphoreType.DMA,
        ],
    )(perm, incident)


def weave_kernel(*refs):
    for q in range(4):
        refs[4][q * 2 * LEAF : (q + 1) * 2 * LEAF, :] = refs[q][...]


def weave(parts):
    return pl.pallas_call(
        weave_kernel,
        out_shape=pltpu.VMEM((8 * LEAF, COLS), BF16),
        in_specs=[VMEM] * 4,
        out_specs=VMEM,
        compiler_params=limit(4),
    )(*parts)


def prepare_kernel(
    rank_ref, far_rows, far_cols, near_rows, near_cols, u_ref, v_ref, u_out, v_out, lists
):
    my_x, my_y, my_z, my_core = position()

    def gray(d):
        return d ^ (d >> 1)

    def entry(b, row, col):
        k = col & (SLAB - 1)
        r = k >> 1
        dx = gray((my_x - (r >> 2)) & 3)
        dy = gray((my_y - (r & 3)) & 3)
        slot = jnp.where(my_core == 0, dy * 4 + dx, dx * 4 + dy) * 2 + (k & 1)
        dz = (((row & (SLAB - 1)) >> 2) - my_z) & 7
        own = 1 - (((row >> 1) & 1) ^ my_core)
        target = ((0x13506427 >> (dz * 4)) & 15) * 4 + own * 2 + (row & 1)
        return b | (slot << 6) | (target << 11)

    def fill(count, rows, cols, base):
        def step(b, carry):
            lists[base + b] = entry(b, rows[b], cols[b])
            return carry

        lax.fori_loop(0, count, step, 0)

    fill(NB, far_rows, far_cols, 0)
    fill(NN, near_rows, near_cols, NB)

    line = lax.broadcasted_iota(jnp.int32, (RMAX, LEAF), 0)

    def step(b, carry):
        keep = line < rank_ref[b]
        for k in range(2):
            v = v_ref[b, k]
            v_out[b, :, k * LEAF : (k + 1) * LEAF] = jnp.where(keep, v.astype(F32), 0.0).astype(BF16)
        u_out[b] = jnp.concatenate([u_ref[b, 0], u_ref[b, 1]], axis=0).T
        return carry

    lax.fori_loop(0, NB, step, 0, unroll=4)


def prepare(rank, far_rows, far_cols, near_rows, near_cols, u, v):
    return pl.pallas_call(
        prepare_kernel,
        out_shape=(
            pltpu.VMEM((NB, LEAF, 2 * RMAX), BF16),
            pltpu.VMEM((NB, RMAX, 2 * LEAF), BF16),
            pltpu.SMEM((NB + NN,), jnp.int32),
        ),
        in_specs=[SMEM] * 5 + [VMEM] * 2,
        out_specs=(VMEM, VMEM, SMEM),
        compiler_params=limit(4),
        cost_estimate=pl.CostEstimate(flops=0, bytes_accessed=8 << 20, transcendentals=0),
    )(rank, far_rows, far_cols, near_rows, near_cols, u, v)


def block_kernel(lists, *refs):
    pieces = refs[:4]
    u_ref, v_ref, near_ref, other_ref, own_ref, trial, total = refs[4:]
    for p, piece in enumerate(pieces):
        for q in range(8):
            x = piece[q * LEAF : (q + 1) * LEAF, :]
            trial[p * 8 + q, :LEAF, :] = x
            trial[p * 8 + q, LEAF:, :] = swap_parts(x)
    total[...] = jnp.zeros_like(total)

    def entries(base, q):
        found = []
        for k in range(WAYS):
            e = lists[base + q * WAYS + k]
            found.append((e & 63, (e >> 6) & 31, e >> 11))
        return found

    def far_step(q, carry):
        found = entries(0, q)
        coeffs = [
            jnp.dot(v_ref[b], trial[slot], preferred_element_type=F32).astype(BF16)
            for b, slot, _ in found
        ]
        for coeff, (b, _, target) in zip(coeffs, found):
            both = jnp.concatenate([coeff, swap_parts(coeff)], axis=0)
            total[target] += jnp.dot(u_ref[b], both, preferred_element_type=F32)
        return carry

    def near_step(q, carry):
        for n, slot, target in entries(NB, q):
            block = jnp.concatenate([near_ref[n, 0], near_ref[n, 1]], axis=1)
            total[target] += jnp.dot(block, trial[slot], preferred_element_type=F32)
        return carry

    lax.fori_loop(0, NB // WAYS, far_step, 0)
    lax.fori_loop(0, NN // WAYS, near_step, 0)

    for j in range(NZ):
        for k in range(2):
            rows = slice((j * 2 + k) * LEAF, (j * 2 + k + 1) * LEAF)
            other_ref[rows, :] = total[j * 4 + k].astype(BF16)
            own_ref[rows, :] = total[j * 4 + 2 + k]


def blocks(lists, pieces, u, v, near):
    rows = NZ * 2 * LEAF
    return pl.pallas_call(
        block_kernel,
        out_shape=(
            pltpu.VMEM((rows, COLS), BF16),
            pltpu.VMEM((rows, COLS), F32),
        ),
        in_specs=[SMEM] + [VMEM] * 7,
        out_specs=(VMEM, VMEM),
        scratch_shapes=[
            pltpu.VMEM((SLAB, 2 * LEAF, COLS), BF16),
            pltpu.VMEM((NZ * 4, LEAF, COLS), F32),
        ],
        compiler_params=limit(12),
        cost_estimate=pl.CostEstimate(
            flops=1 << 30, bytes_accessed=16 << 20, transcendentals=0
        ),
    )(lists, *pieces, u, v, near)


def gather(mine):
    two, back, ahead = [hop(0, step, mine) for step in (2, -1, 1)]
    first = weave([mine, ahead, back, two])
    two, back, ahead = [hop(1, step, first) for step in (2, -1, 1)]
    return [first, ahead, back, two]


def body(
    incident, perm, far_u, far_v, far_rank, far_rows, far_cols, near_block, near_rows, near_cols
):
    mine = order(perm, incident)
    u, v, lists = prepare(
        far_rank,
        far_rows,
        far_cols,
        near_rows,
        near_cols,
        jnp.swapaxes(far_u, 2, 3),
        jnp.swapaxes(far_v, 2, 3),
    )
    pieces = gather(mine)
    other, own = blocks(lists, pieces, u, v, near_block)
    swapped = other_core(other)
    total, parts = None, []
    for j, step in enumerate(STEPS):
        rows = slice(j * 2 * LEAF, (j + 1) * 2 * LEAF)
        chip = own[rows] + swapped[rows].astype(F32)
        if step == 0:
            total = chip
        else:
            parts.append(along_z(step, chip.astype(BF16)))
    for part in parts:
        total = total + part.astype(F32)
    return total.astype(BF16)


def solution(mesh):
    placed = (
        P(("col", "row"), None),
        P(("col", "row"), None),
        P(("row", "col"), None, None, None),
        P(("row", "col"), None, None, None),
        P(("row", "col")),
        P(("row", "col")),
        P(("row", "col")),
        P(("row", "col"), None, None, None),
        P(("row", "col")),
        P(("row", "col")),
    )
    return jax.shard_map(
        body, mesh=mesh, in_specs=placed, out_specs=P(("row", "col"), None), check_vma=False
    )
```

```python
import jax
import jax.numpy as jnp
from jax import lax
from jax.experimental import pallas as pl
from jax.experimental.pallas import tpu as pltpu
from jax.sharding import PartitionSpec as P

LEAF = 128
COLS = 256
HALF = 128
RMAX = 64
NB = 32
NN = 28
NX = 4
NY = 4
NZ = 8
NCORE = 2
SLAB = 32
WAYS = 4
GROUPS = 4
LIST = 36
COUNTS = 2 * GROUPS * LIST
ORDER_OF_STEP = 0x13506427
STEPS = (4, 7, 1, 6, 2, 5, 3, 0)
F32 = jnp.float32
BF16 = jnp.bfloat16
VMEM = pl.BlockSpec(memory_space=pltpu.VMEM)
SMEM = pl.BlockSpec(memory_space=pltpu.SMEM)
ANY = pl.BlockSpec(memory_space=pl.ANY)


def limit(mib):
    return pltpu.CompilerParams(vmem_limit_bytes=mib << 20)


def position():
    row, col = lax.axis_index("row"), lax.axis_index("col")
    return row // NY, row % NY, col // NCORE, col % NCORE


def hop(turn, step, value):
    pairs = []
    for d in range(NX * NY * NZ * NCORE):
        row, col = divmod(d, NZ * NCORE)
        x, y = divmod(row, NY)
        if (col + turn) % NCORE == 0:
            x = (x + step) % NX
        else:
            y = (y + step) % NY
        pairs.append((d, (x * NY + y) * NZ * NCORE + col))
    return lax.ppermute(value, ("row", "col"), pairs)


def along_z(step, value):
    pairs = [
        (z * NCORE + c, (z + step) % NZ * NCORE + c) for z in range(NZ) for c in range(NCORE)
    ]
    return lax.ppermute(value, "col", pairs)


def other_core(value):
    return lax.ppermute(value, "col", [(d, d ^ 1) for d in range(NZ * NCORE)])


def after(value, earlier):
    return lax.optimization_barrier((value, earlier))[0]


def swap_parts(values):
    return jnp.concatenate([-values[:, HALF:], values[:, :HALF]], axis=1)


def order_kernel(perm_hbm, x_hbm, out_ref, perm_ref, x_ref, perm_sem, x_sem):
    x_copy = pltpu.make_async_copy(x_hbm, x_ref, x_sem)
    perm_copy = pltpu.make_async_copy(perm_hbm, perm_ref, perm_sem)
    x_copy.start()
    perm_copy.start()
    source = lax.broadcasted_iota(jnp.int32, (LEAF, LEAF), 0)
    perm_copy.wait()
    x_copy.wait()
    for k in range(2):
        rows = slice(k * LEAF, (k + 1) * LEAF)
        chosen = (source == perm_ref[k : k + 1, :]).astype(F32).astype(BF16)
        out_ref[rows, :] = lax.dot_general(
            chosen, x_ref[rows, :], (((0,), (0,)), ((), ())), preferred_element_type=F32
        ).astype(BF16)


def order(perm, incident):
    return pl.pallas_call(
        order_kernel,
        out_shape=pltpu.VMEM((2 * LEAF, COLS), BF16),
        in_specs=[ANY, ANY],
        out_specs=VMEM,
        scratch_shapes=[
            pltpu.VMEM((2, LEAF), jnp.int32),
            pltpu.VMEM((2 * LEAF, COLS), BF16),
            pltpu.SemaphoreType.DMA,
            pltpu.SemaphoreType.DMA,
        ],
    )(perm, incident)


def weave_kernel(*refs):
    for q in range(4):
        refs[4][q * 2 * LEAF : (q + 1) * 2 * LEAF, :] = refs[q][...]


def weave(parts):
    return pl.pallas_call(
        weave_kernel,
        out_shape=pltpu.VMEM((8 * LEAF, COLS), BF16),
        in_specs=[VMEM] * 4,
        out_specs=VMEM,
        compiler_params=limit(4),
    )(*parts)


def prepare_kernel(
    rank_hbm,
    far_rows_hbm,
    far_cols_hbm,
    near_rows_hbm,
    near_cols_hbm,
    u_hbm,
    v_hbm,
    u_out,
    v_out,
    lists,
    rank,
    far_rows,
    far_cols,
    near_rows,
    near_cols,
    u_ref,
    v_ref,
    sems,
):
    pairs = (
        (far_rows_hbm, far_rows),
        (far_cols_hbm, far_cols),
        (near_rows_hbm, near_rows),
        (near_cols_hbm, near_cols),
        (rank_hbm, rank),
        (v_hbm, v_ref),
        (u_hbm, u_ref),
    )
    copies = [pltpu.make_async_copy(a, b, sems.at[k]) for k, (a, b) in enumerate(pairs)]
    for copy in copies:
        copy.start()
    my_x, my_y, my_z, my_core = position()

    def gray(d):
        return d ^ (d >> 1)

    def entry(b, row, col):
        k = col & (SLAB - 1)
        r = k >> 1
        dx = gray((my_x - (r >> 2)) & 3)
        dy = gray((my_y - (r & 3)) & 3)
        piece = jnp.where(my_core == 0, dy, dx)
        place = jnp.where(my_core == 0, dx, dy) * 2 + (k & 1)
        dz = (((row & (SLAB - 1)) >> 2) - my_z) & 7
        own = 1 - (((row >> 1) & 1) ^ my_core)
        target = own * 16 + ((ORDER_OF_STEP >> (dz * 4)) & 15) * 2 + (row & 1)
        late = (piece == 1) | (piece == 2)
        group = jnp.where(late, 2 + own, jnp.where(piece == 0, 0, 1))
        slot = jnp.where(piece == 2, 8 + place, place)
        return group, b | (slot << 6) | (target << 11)

    def fill(count, rows, cols, kind):
        for g in range(GROUPS):
            lists[COUNTS + kind * GROUPS + g] = 0

        def step(b, carry):
            group, value = entry(b, rows[b], cols[b])
            at = COUNTS + kind * GROUPS + group
            used = lists[at]
            lists[(kind * GROUPS + group) * LIST + used] = value
            lists[at] = used + 1
            return carry

        lax.fori_loop(0, count, step, 0)
        for g in range(GROUPS):
            at = COUNTS + kind * GROUPS + g
            used = lists[at]
            for k in range(WAYS - 1):
                lists[(kind * GROUPS + g) * LIST + used + k] = SLAB << 11
            lists[at] = (used + WAYS - 1) // WAYS

    for copy in copies[:4]:
        copy.wait()
    fill(NB, far_rows, far_cols, 0)
    fill(NN, near_rows, near_cols, 1)
    for copy in copies[4:]:
        copy.wait()
    line = lax.broadcasted_iota(jnp.int32, (RMAX, LEAF), 0)

    def step(b, carry):
        keep = line < rank[b]
        for k in range(2):
            v = v_ref[b, k]
            v_out[b, :, k * LEAF : (k + 1) * LEAF] = jnp.where(keep, v.astype(F32), 0.0).astype(BF16)
        u_out[b] = jnp.concatenate([u_ref[b, 0], u_ref[b, 1]], axis=0).T
        return carry

    lax.fori_loop(0, NB, step, 0, unroll=4)


def prepare(rank, far_rows, far_cols, near_rows, near_cols, u, v):
    operands = (rank, far_rows, far_cols, near_rows, near_cols, u, v)
    operands = [pltpu.with_memory_space_constraint(x, pltpu.HBM) for x in operands]
    return pl.pallas_call(
        prepare_kernel,
        out_shape=(
            pltpu.VMEM((NB, LEAF, 2 * RMAX), BF16),
            pltpu.VMEM((NB, RMAX, 2 * LEAF), BF16),
            pltpu.SMEM((COUNTS + 2 * GROUPS,), jnp.int32),
        ),
        in_specs=[ANY] * 7,
        out_specs=(VMEM, VMEM, SMEM),
        scratch_shapes=[
            pltpu.SMEM((NB,), jnp.int32),
            pltpu.SMEM((NB,), jnp.int32),
            pltpu.SMEM((NB,), jnp.int32),
            pltpu.SMEM((NN,), jnp.int32),
            pltpu.SMEM((NN,), jnp.int32),
            pltpu.VMEM((NB, 2, RMAX, LEAF), BF16),
            pltpu.VMEM((NB, 2, RMAX, LEAF), BF16),
            pltpu.SemaphoreType.DMA((7,)),
        ],
        compiler_params=limit(4),
        cost_estimate=cost(8),
    )(*operands)


def cost(mib):
    return pl.CostEstimate(flops=0, bytes_accessed=mib << 20, transcendentals=0)


def load(piece, trial, base):
    for q in range(8):
        x = piece[q * LEAF : (q + 1) * LEAF, :]
        trial[base + q, :LEAF, :] = x
        trial[base + q, LEAF:, :] = swap_parts(x)


def work(group, lists, u_ref, v_ref, near_ref, trial, total):
    def entries(kind, q):
        found = []
        for k in range(WAYS):
            e = lists[(kind * GROUPS + group) * LIST + q * WAYS + k]
            found.append((e & 63, (e >> 6) & 31, e >> 11))
        return found

    def far_step(q, carry):
        found = entries(0, q)
        coeffs = [
            jnp.dot(v_ref[b], trial[slot], preferred_element_type=F32).astype(BF16)
            for b, slot, _ in found
        ]
        for coeff, (b, _, target) in zip(coeffs, found):
            both = jnp.concatenate([coeff, swap_parts(coeff)], axis=0)
            total[target] += jnp.dot(u_ref[b], both, preferred_element_type=F32)
        return carry

    def near_step(q, carry):
        for n, slot, target in entries(1, q):
            block = jnp.concatenate([near_ref[n, 0], near_ref[n, 1]], axis=1)
            total[target] += jnp.dot(block, trial[slot], preferred_element_type=F32)
        return carry

    lax.fori_loop(0, lists[COUNTS + group], far_step, 0)
    lax.fori_loop(0, lists[COUNTS + GROUPS + group], near_step, 0)


TOTAL = pltpu.VMEM((SLAB + 1, LEAF, COLS), F32)


def first_kernel(lists, u_ref, v_ref, near_ref, piece, total, trial):
    total[...] = jnp.zeros_like(total)
    load(piece, trial, 0)
    work(0, lists, u_ref, v_ref, near_ref, trial, total)


def second_kernel(lists, u_ref, v_ref, near_ref, piece, _, total, trial):
    load(piece, trial, 0)
    work(1, lists, u_ref, v_ref, near_ref, trial, total)


def third_kernel(lists, u_ref, v_ref, near_ref, ahead, back, _, total, trial, other_ref):
    load(ahead, trial, 0)
    load(back, trial, 8)
    work(2, lists, u_ref, v_ref, near_ref, trial, total)
    for t in range(SLAB // 2):
        other_ref[t * LEAF : (t + 1) * LEAF, :] = total[t].astype(BF16)


def fourth_kernel(lists, u_ref, v_ref, near_ref, trial, _, total):
    work(3, lists, u_ref, v_ref, near_ref, trial, total)


def blocks(common, pieces):
    first, ahead, back, two = pieces
    scratch = [pltpu.VMEM((8, 2 * LEAF, COLS), BF16)]
    total = pl.pallas_call(
        first_kernel,
        out_shape=TOTAL,
        in_specs=[SMEM] + [VMEM] * 4,
        out_specs=VMEM,
        scratch_shapes=scratch,
        compiler_params=limit(6),
        cost_estimate=cost(8),
    )(*common, first)
    total = pl.pallas_call(
        second_kernel,
        out_shape=TOTAL,
        in_specs=[SMEM] + [VMEM] * 5,
        out_specs=VMEM,
        scratch_shapes=scratch,
        input_output_aliases={5: 0},
        compiler_params=limit(6),
        cost_estimate=cost(6),
    )(*common, two, total)
    total, trial, other = pl.pallas_call(
        third_kernel,
        out_shape=(
            TOTAL,
            pltpu.VMEM((16, 2 * LEAF, COLS), BF16),
            pltpu.VMEM((SLAB // 2 * LEAF, COLS), BF16),
        ),
        in_specs=[SMEM] + [VMEM] * 6,
        out_specs=(VMEM, VMEM, VMEM),
        input_output_aliases={6: 0},
        compiler_params=limit(6),
        cost_estimate=cost(8),
    )(*common, ahead, back, total)
    total = pl.pallas_call(
        fourth_kernel,
        out_shape=TOTAL,
        in_specs=[SMEM] + [VMEM] * 5,
        out_specs=VMEM,
        input_output_aliases={5: 0},
        compiler_params=limit(6),
        cost_estimate=cost(6),
    )(*common, trial, total)
    return other, total


def gather(mine):
    two, back, ahead = [hop(0, step, mine) for step in (2, -1, 1)]
    first = weave([mine, ahead, back, two])
    two, back, ahead = [hop(1, step, first) for step in (2, -1, 1)]
    return [first, ahead, back, two]


def body(
    incident, perm, far_u, far_v, far_rank, far_rows, far_cols, near_block, near_rows, near_cols
):
    mine = order(perm, incident)
    u, v, lists = prepare(
        far_rank,
        far_rows,
        far_cols,
        near_rows,
        near_cols,
        jnp.swapaxes(far_u, 2, 3),
        jnp.swapaxes(far_v, 2, 3),
    )
    pieces = gather(mine)
    other, own = blocks((lists, u, v, near_block), pieces)
    swapped = other_core(other)
    total, parts = None, []
    for j, step in enumerate(STEPS):
        rows = slice(j * 2 * LEAF, (j + 1) * 2 * LEAF)
        mine = own[SLAB // 2 + 2 * j : SLAB // 2 + 2 * j + 2].reshape(2 * LEAF, COLS)
        chip = mine + swapped[rows].astype(F32)
        if step == 0:
            total = chip
        else:
            parts.append(along_z(step, chip.astype(BF16)))
    for part in parts:
        total = total + part.astype(F32)
    return total.astype(BF16)


def solution(mesh):
    placed = (
        P(("col", "row"), None),
        P(("col", "row"), None),
        P(("row", "col"), None, None, None),
        P(("row", "col"), None, None, None),
        P(("row", "col")),
        P(("row", "col")),
        P(("row", "col")),
        P(("row", "col"), None, None, None),
        P(("row", "col")),
        P(("row", "col")),
    )
    return jax.shard_map(
        body, mesh=mesh, in_specs=placed, out_specs=P(("row", "col"), None), check_vma=False
    )
```

```python
import jax
import jax.numpy as jnp
from jax import lax
from jax.experimental import pallas as pl
from jax.experimental.pallas import tpu as pltpu
from jax.sharding import PartitionSpec as P

LEAF = 128
COLS = 256
HALF = 128
RMAX = 64
NB = 32
NN = 28
NX = 4
NY = 4
NZ = 8
NCORE = 2
SLAB = 32
WAYS = 4
GROUPS = 4
LIST = 36
COUNTS = 2 * GROUPS * LIST
F32 = jnp.float32
BF16 = jnp.bfloat16
VMEM = pl.BlockSpec(memory_space=pltpu.VMEM)
SMEM = pl.BlockSpec(memory_space=pltpu.SMEM)
ANY = pl.BlockSpec(memory_space=pl.ANY)


def limit(mib):
    return pltpu.CompilerParams(vmem_limit_bytes=mib << 20)


def position():
    row, col = lax.axis_index("row"), lax.axis_index("col")
    return row // NY, row % NY, col // NCORE, col % NCORE


def hop(turn, step, value):
    pairs = []
    for d in range(NX * NY * NZ * NCORE):
        row, col = divmod(d, NZ * NCORE)
        x, y = divmod(row, NY)
        if (col + turn) % NCORE == 0:
            x = (x + step) % NX
        else:
            y = (y + step) % NY
        pairs.append((d, (x * NY + y) * NZ * NCORE + col))
    return lax.ppermute(value, ("row", "col"), pairs)


def along_z(step, value, turn=0):
    pairs = []
    for d in range(NZ * NCORE):
        z, c = divmod(d, NCORE)
        z = (z + step * (1 - 2 * c)) % NZ
        pairs.append((d, z * NCORE + (c + turn) % NCORE))
    return lax.ppermute(value, "col", pairs)


def other_core(value):
    return lax.ppermute(value, "col", [(d, d ^ 1) for d in range(NZ * NCORE)])


def after(value, earlier):
    return lax.optimization_barrier((value, earlier))[0]


def swap_parts(values):
    return jnp.concatenate([-values[:, HALF:], values[:, :HALF]], axis=1)


def order_kernel(perm_hbm, x_hbm, out_ref, perm_ref, x_ref, perm_sem, x_sem):
    x_copy = pltpu.make_async_copy(x_hbm, x_ref, x_sem)
    perm_copy = pltpu.make_async_copy(perm_hbm, perm_ref, perm_sem)
    x_copy.start()
    perm_copy.start()
    source = lax.broadcasted_iota(jnp.int32, (LEAF, LEAF), 0)
    perm_copy.wait()
    x_copy.wait()
    for k in range(2):
        rows = slice(k * LEAF, (k + 1) * LEAF)
        chosen = (source == perm_ref[k : k + 1, :]).astype(F32).astype(BF16)
        out_ref[rows, :] = lax.dot_general(
            chosen, x_ref[rows, :], (((0,), (0,)), ((), ())), preferred_element_type=F32
        ).astype(BF16)


def order(perm, incident):
    return pl.pallas_call(
        order_kernel,
        out_shape=pltpu.VMEM((2 * LEAF, COLS), BF16),
        in_specs=[ANY, ANY],
        out_specs=VMEM,
        scratch_shapes=[
            pltpu.VMEM((2, LEAF), jnp.int32),
            pltpu.VMEM((2 * LEAF, COLS), BF16),
            pltpu.SemaphoreType.DMA,
            pltpu.SemaphoreType.DMA,
        ],
    )(perm, incident)


def weave_kernel(*refs):
    for q in range(4):
        refs[4][q * 2 * LEAF : (q + 1) * 2 * LEAF, :] = refs[q][...]


def weave(parts):
    return pl.pallas_call(
        weave_kernel,
        out_shape=pltpu.VMEM((8 * LEAF, COLS), BF16),
        in_specs=[VMEM] * 4,
        out_specs=VMEM,
        compiler_params=limit(4),
    )(*parts)


def prepare_kernel(
    rank_hbm,
    far_rows_hbm,
    far_cols_hbm,
    near_rows_hbm,
    near_cols_hbm,
    u_hbm,
    v_hbm,
    u_out,
    v_out,
    lists,
    rank,
    far_rows,
    far_cols,
    near_rows,
    near_cols,
    u_ref,
    v_ref,
    sems,
):
    pairs = (
        (far_rows_hbm, far_rows),
        (far_cols_hbm, far_cols),
        (near_rows_hbm, near_rows),
        (near_cols_hbm, near_cols),
        (rank_hbm, rank),
        (v_hbm, v_ref),
        (u_hbm, u_ref),
    )
    copies = [pltpu.make_async_copy(a, b, sems.at[k]) for k, (a, b) in enumerate(pairs)]
    for copy in copies:
        copy.start()
    my_x, my_y, my_z, my_core = position()

    def gray(d):
        return d ^ (d >> 1)

    def entry(b, row, col):
        k = col & (SLAB - 1)
        r = k >> 1
        dx = gray((my_x - (r >> 2)) & 3)
        dy = gray((my_y - (r & 3)) & 3)
        piece = jnp.where(my_core == 0, dy, dx)
        place = jnp.where(my_core == 0, dx, dy) * 2 + (k & 1)
        i, owner = row & 1, (row >> 1) & 1
        dz = (((row & (SLAB - 1)) >> 2) - my_z) & 7
        straight = (dz & 3) == 0
        handler = jnp.where(straight, owner, dz >> 2)
        steps = jnp.where(handler == 0, dz, 8 - dz)
        near = jnp.where(straight, 14 - 14 * (dz >> 2) + i, 14 - 4 * steps + owner * 2 + i)
        own = jnp.where(handler == my_core, 1, 0)
        target = own * 16 + near
        late = (piece == 1) | (piece == 2)
        group = jnp.where(late, 2 + own, jnp.where(piece == 0, 0, 1))
        slot = jnp.where(piece == 2, 8 + place, place)
        return group, b | (slot << 6) | (target << 11)

    def fill(count, rows, cols, kind):
        for g in range(GROUPS):
            lists[COUNTS + kind * GROUPS + g] = 0

        def step(b, carry):
            group, value = entry(b, rows[b], cols[b])
            at = COUNTS + kind * GROUPS + group
            used = lists[at]
            lists[(kind * GROUPS + group) * LIST + used] = value
            lists[at] = used + 1
            return carry

        lax.fori_loop(0, count, step, 0)
        for g in range(GROUPS):
            at = COUNTS + kind * GROUPS + g
            used = lists[at]
            for k in range(WAYS - 1):
                lists[(kind * GROUPS + g) * LIST + used + k] = SLAB << 11
            lists[at] = (used + WAYS - 1) // WAYS

    for copy in copies[:4]:
        copy.wait()
    fill(NB, far_rows, far_cols, 0)
    fill(NN, near_rows, near_cols, 1)
    for copy in copies[4:]:
        copy.wait()
    line = lax.broadcasted_iota(jnp.int32, (RMAX, LEAF), 0)

    def step(b, carry):
        keep = line < rank[b]
        for k in range(2):
            v = v_ref[b, k]
            v_out[b, :, k * LEAF : (k + 1) * LEAF] = jnp.where(keep, v.astype(F32), 0.0).astype(BF16)
        u_out[b] = jnp.concatenate([u_ref[b, 0], u_ref[b, 1]], axis=0).T
        return carry

    lax.fori_loop(0, NB, step, 0, unroll=4)


def prepare(rank, far_rows, far_cols, near_rows, near_cols, u, v):
    operands = (rank, far_rows, far_cols, near_rows, near_cols, u, v)
    operands = [pltpu.with_memory_space_constraint(x, pltpu.HBM) for x in operands]
    return pl.pallas_call(
        prepare_kernel,
        out_shape=(
            pltpu.VMEM((NB, LEAF, 2 * RMAX), BF16),
            pltpu.VMEM((NB, RMAX, 2 * LEAF), BF16),
            pltpu.SMEM((COUNTS + 2 * GROUPS,), jnp.int32),
        ),
        in_specs=[ANY] * 7,
        out_specs=(VMEM, VMEM, SMEM),
        scratch_shapes=[
            pltpu.SMEM((NB,), jnp.int32),
            pltpu.SMEM((NB,), jnp.int32),
            pltpu.SMEM((NB,), jnp.int32),
            pltpu.SMEM((NN,), jnp.int32),
            pltpu.SMEM((NN,), jnp.int32),
            pltpu.VMEM((NB, 2, RMAX, LEAF), BF16),
            pltpu.VMEM((NB, 2, RMAX, LEAF), BF16),
            pltpu.SemaphoreType.DMA((7,)),
        ],
        compiler_params=limit(4),
        cost_estimate=cost(8),
    )(*operands)


def cost(mib):
    return pl.CostEstimate(flops=0, bytes_accessed=mib << 20, transcendentals=0)


def load(piece, trial, base):
    for q in range(8):
        x = piece[q * LEAF : (q + 1) * LEAF, :]
        trial[base + q, :LEAF, :] = x
        trial[base + q, LEAF:, :] = swap_parts(x)


def work(group, lists, u_ref, v_ref, near_ref, trial, total):
    def entries(kind, q):
        found = []
        for k in range(WAYS):
            e = lists[(kind * GROUPS + group) * LIST + q * WAYS + k]
            found.append((e & 63, (e >> 6) & 31, e >> 11))
        return found

    def far_step(q, carry):
        found = entries(0, q)
        coeffs = [
            jnp.dot(v_ref[b], trial[slot], preferred_element_type=F32).astype(BF16)
            for b, slot, _ in found
        ]
        for coeff, (b, _, target) in zip(coeffs, found):
            both = jnp.concatenate([coeff, swap_parts(coeff)], axis=0)
            total[target] += jnp.dot(u_ref[b], both, preferred_element_type=F32)
        return carry

    def near_step(q, carry):
        for n, slot, target in entries(1, q):
            block = jnp.concatenate([near_ref[n, 0], near_ref[n, 1]], axis=1)
            total[target] += jnp.dot(block, trial[slot], preferred_element_type=F32)
        return carry

    lax.fori_loop(0, lists[COUNTS + group], far_step, 0)
    lax.fori_loop(0, lists[COUNTS + GROUPS + group], near_step, 0)


TOTAL = pltpu.VMEM((SLAB + 1, LEAF, COLS), F32)


def first_kernel(lists, u_ref, v_ref, near_ref, piece, total, trial):
    total[...] = jnp.zeros_like(total)
    load(piece, trial, 0)
    work(0, lists, u_ref, v_ref, near_ref, trial, total)


def second_kernel(lists, u_ref, v_ref, near_ref, piece, _, total, trial):
    load(piece, trial, 0)
    work(1, lists, u_ref, v_ref, near_ref, trial, total)


def third_kernel(lists, u_ref, v_ref, near_ref, ahead, back, _, total, trial, other_ref):
    load(ahead, trial, 0)
    load(back, trial, 8)
    work(2, lists, u_ref, v_ref, near_ref, trial, total)
    for t in range(SLAB // 2):
        other_ref[t * LEAF : (t + 1) * LEAF, :] = total[t].astype(BF16)


def fourth_kernel(lists, u_ref, v_ref, near_ref, trial, _, total):
    work(3, lists, u_ref, v_ref, near_ref, trial, total)


def blocks(common, pieces):
    first, ahead, back, two = pieces
    scratch = [pltpu.VMEM((8, 2 * LEAF, COLS), BF16)]
    total = pl.pallas_call(
        first_kernel,
        out_shape=TOTAL,
        in_specs=[SMEM] + [VMEM] * 4,
        out_specs=VMEM,
        scratch_shapes=scratch,
        compiler_params=limit(6),
        cost_estimate=cost(8),
    )(*common, first)
    total = pl.pallas_call(
        second_kernel,
        out_shape=TOTAL,
        in_specs=[SMEM] + [VMEM] * 5,
        out_specs=VMEM,
        scratch_shapes=scratch,
        input_output_aliases={5: 0},
        compiler_params=limit(6),
        cost_estimate=cost(6),
    )(*common, two, total)
    total, trial, other = pl.pallas_call(
        third_kernel,
        out_shape=(
            TOTAL,
            pltpu.VMEM((16, 2 * LEAF, COLS), BF16),
            pltpu.VMEM((SLAB // 2 * LEAF, COLS), BF16),
        ),
        in_specs=[SMEM] + [VMEM] * 6,
        out_specs=(VMEM, VMEM, VMEM),
        input_output_aliases={6: 0},
        compiler_params=limit(6),
        cost_estimate=cost(8),
    )(*common, ahead, back, total)
    total = pl.pallas_call(
        fourth_kernel,
        out_shape=TOTAL,
        in_specs=[SMEM] + [VMEM] * 5,
        out_specs=VMEM,
        input_output_aliases={5: 0},
        compiler_params=limit(6),
        cost_estimate=cost(6),
    )(*common, trial, total)
    return other, total


def gather(mine):
    two, back, ahead = [hop(0, step, mine) for step in (2, -1, 1)]
    first = weave([mine, ahead, back, two])
    two, back, ahead = [hop(1, step, first) for step in (2, -1, 1)]
    return [first, ahead, back, two]


def chip_sum(own, swapped, first, count):
    mine = own[SLAB // 2 + first : SLAB // 2 + first + count].reshape(count * LEAF, COLS)
    return mine + swapped[first * LEAF : (first + count) * LEAF].astype(F32)


def cluster(k):
    return pl.ds(pl.multiple_of(k * LEAF, LEAF), LEAF)


def relay_kernel(own, swapped, close, middle, same_ref, cross_ref):
    core = position()[3]
    for owner, out in ((core, same_ref), (1 - core, cross_ref)):
        for i in range(2):
            place = owner * 2 + i

            total = own[SLAB // 2 + 10 + place] + swapped[cluster(10 + place), :].astype(F32)
            total += close[cluster(place), :].astype(F32) + middle[cluster(2 + place), :].astype(F32)
            out[i * LEAF : (i + 1) * LEAF, :] = total.astype(BF16)


def relay(own, swapped, close, middle):
    shape = pltpu.VMEM((2 * LEAF, COLS), BF16)
    return pl.pallas_call(
        relay_kernel,
        out_shape=(shape, shape),
        in_specs=[VMEM] * 4,
        out_specs=(VMEM, VMEM),
        compiler_params=limit(4),
    )(own, swapped, close, middle)


def scatter(swapped, own):
    middle = along_z(2, chip_sum(own, swapped, 0, 6).astype(BF16))
    close = along_z(1, chip_sum(own, swapped, 6, 4).astype(BF16))
    same, cross = relay(own, swapped, close, middle)
    far = after(middle[: 2 * LEAF], same)
    same, cross = along_z(1, same), along_z(1, cross, 1)
    far = along_z(2, far)
    total = chip_sum(own, swapped, 14, 2) + far.astype(F32)
    return (total + same.astype(F32) + cross.astype(F32)).astype(BF16)


def body(
    incident, perm, far_u, far_v, far_rank, far_rows, far_cols, near_block, near_rows, near_cols
):
    mine = order(perm, incident)
    u, v, lists = prepare(
        far_rank,
        far_rows,
        far_cols,
        near_rows,
        near_cols,
        jnp.swapaxes(far_u, 2, 3),
        jnp.swapaxes(far_v, 2, 3),
    )
    pieces = gather(mine)
    other, own = blocks((lists, u, v, near_block), pieces)
    return scatter(other_core(other), own)


def solution(mesh):
    placed = (
        P(("col", "row"), None),
        P(("col", "row"), None),
        P(("row", "col"), None, None, None),
        P(("row", "col"), None, None, None),
        P(("row", "col")),
        P(("row", "col")),
        P(("row", "col")),
        P(("row", "col"), None, None, None),
        P(("row", "col")),
        P(("row", "col")),
    )
    return jax.shard_map(
        body, mesh=mesh, in_specs=placed, out_specs=P(("row", "col"), None), check_vma=False
    )
```

```python
import jax
import jax.numpy as jnp
from jax import lax
from jax.experimental import pallas as pl
from jax.experimental.pallas import tpu as pltpu
from jax.sharding import PartitionSpec as P

LEAF = 128
COLS = 256
HALF = 128
RMAX = 64
NB = 32
NN = 28
NX = 4
NY = 4
NZ = 8
NCORE = 2
SLAB = 32
WAYS = 4
GROUPS = 4
LIST = 36
COUNTS = 2 * GROUPS * LIST
FIRST = 6
F32 = jnp.float32
BF16 = jnp.bfloat16
VMEM = pl.BlockSpec(memory_space=pltpu.VMEM)
SMEM = pl.BlockSpec(memory_space=pltpu.SMEM)
ANY = pl.BlockSpec(memory_space=pl.ANY)


def limit(mib):
    return pltpu.CompilerParams(vmem_limit_bytes=mib << 20)


def position():
    row, col = lax.axis_index("row"), lax.axis_index("col")
    return row // NY, row % NY, col // NCORE, col % NCORE


def hop(turn, step, value):
    pairs = []
    for d in range(NX * NY * NZ * NCORE):
        row, col = divmod(d, NZ * NCORE)
        x, y = divmod(row, NY)
        if (col + turn) % NCORE == 0:
            x = (x + step) % NX
        else:
            y = (y + step) % NY
        pairs.append((d, (x * NY + y) * NZ * NCORE + col))
    return lax.ppermute(value, ("row", "col"), pairs)


def along_z(step, value, turn=0):
    pairs = []
    for d in range(NZ * NCORE):
        z, c = divmod(d, NCORE)
        z = (z + step * (1 - 2 * c)) % NZ
        pairs.append((d, z * NCORE + (c + turn) % NCORE))
    return lax.ppermute(value, "col", pairs)


def other_core(value):
    return lax.ppermute(value, "col", [(d, d ^ 1) for d in range(NZ * NCORE)])


def after(value, earlier):
    return lax.optimization_barrier((value, earlier))[0]


def swap_parts(values):
    return jnp.concatenate([-values[:, HALF:], values[:, :HALF]], axis=1)


def order_kernel(perm_hbm, x_hbm, out_ref, perm_ref, x_ref, perm_sem, x_sem):
    x_copy = pltpu.make_async_copy(x_hbm, x_ref, x_sem)
    perm_copy = pltpu.make_async_copy(perm_hbm, perm_ref, perm_sem)
    x_copy.start()
    perm_copy.start()
    source = lax.broadcasted_iota(jnp.int32, (LEAF, LEAF), 0)
    perm_copy.wait()
    x_copy.wait()
    for k in range(2):
        rows = slice(k * LEAF, (k + 1) * LEAF)
        chosen = (source == perm_ref[k : k + 1, :]).astype(F32).astype(BF16)
        out_ref[rows, :] = lax.dot_general(
            chosen, x_ref[rows, :], (((0,), (0,)), ((), ())), preferred_element_type=F32
        ).astype(BF16)


def order(perm, incident):
    return pl.pallas_call(
        order_kernel,
        out_shape=pltpu.VMEM((2 * LEAF, COLS), BF16),
        in_specs=[ANY, ANY],
        out_specs=VMEM,
        scratch_shapes=[
            pltpu.VMEM((2, LEAF), jnp.int32),
            pltpu.VMEM((2 * LEAF, COLS), BF16),
            pltpu.SemaphoreType.DMA,
            pltpu.SemaphoreType.DMA,
        ],
    )(perm, incident)


def weave_kernel(*refs):
    for q in range(4):
        refs[4][q * 2 * LEAF : (q + 1) * 2 * LEAF, :] = refs[q][...]


def weave(parts):
    return pl.pallas_call(
        weave_kernel,
        out_shape=pltpu.VMEM((8 * LEAF, COLS), BF16),
        in_specs=[VMEM] * 4,
        out_specs=VMEM,
        compiler_params=limit(4),
    )(*parts)


def prepare_kernel(
    rank_hbm,
    far_rows_hbm,
    far_cols_hbm,
    near_rows_hbm,
    near_cols_hbm,
    u_hbm,
    v_hbm,
    u_out,
    v_out,
    lists,
    rank,
    far_rows,
    far_cols,
    near_rows,
    near_cols,
    u_ref,
    v_ref,
    sems,
):
    pairs = (
        (far_rows_hbm, far_rows),
        (far_cols_hbm, far_cols),
        (near_rows_hbm, near_rows),
        (near_cols_hbm, near_cols),
        (rank_hbm, rank),
        (v_hbm, v_ref),
        (u_hbm, u_ref),
    )
    copies = [pltpu.make_async_copy(a, b, sems.at[k]) for k, (a, b) in enumerate(pairs)]
    for copy in copies:
        copy.start()
    my_x, my_y, my_z, my_core = position()

    def gray(d):
        return d ^ (d >> 1)

    def entry(b, row, col):
        k = col & (SLAB - 1)
        r = k >> 1
        dx = gray((my_x - (r >> 2)) & 3)
        dy = gray((my_y - (r & 3)) & 3)
        piece = jnp.where(my_core == 0, dy, dx)
        place = jnp.where(my_core == 0, dx, dy) * 2 + (k & 1)
        i, owner = row & 1, (row >> 1) & 1
        dz = (((row & (SLAB - 1)) >> 2) - my_z) & 7
        straight = (dz & 3) == 0
        handler = jnp.where(straight, owner, dz >> 2)
        steps = jnp.where(handler == 0, dz, 8 - dz)
        near = jnp.where(straight, 14 - 14 * (dz >> 2) + i, 14 - 4 * steps + owner * 2 + i)
        own = jnp.where(handler == my_core, 1, 0)
        target = own * 16 + near
        late = (piece == 1) | (piece == 2)
        group = jnp.where(late, 2 + own, jnp.where(piece == 0, 0, 1))
        slot = jnp.where(piece == 2, 8 + place, place)
        return group, b | (slot << 6) | (target << 11)

    def fill(count, rows, cols, kind):
        for g in range(GROUPS):
            lists[COUNTS + kind * GROUPS + g] = 0

        def step(b, carry):
            group, value = entry(b, rows[b], cols[b])
            at = COUNTS + kind * GROUPS + group
            used = lists[at]
            lists[(kind * GROUPS + group) * LIST + used] = value
            lists[at] = used + 1
            return carry

        lax.fori_loop(0, count, step, 0)
        for g in range(GROUPS):
            at = COUNTS + kind * GROUPS + g
            used = lists[at]
            for k in range(WAYS - 1):
                lists[(kind * GROUPS + g) * LIST + used + k] = SLAB << 11
            lists[at] = (used + WAYS - 1) // WAYS

    for copy in copies[:4]:
        copy.wait()
    fill(NB, far_rows, far_cols, 0)
    fill(NN, near_rows, near_cols, 1)
    for copy in copies[4:]:
        copy.wait()
    line = lax.broadcasted_iota(jnp.int32, (RMAX, LEAF), 0)

    def step(b, carry):
        keep = line < rank[b]
        for k in range(2):
            v = v_ref[b, k]
            v_out[b, :, k * LEAF : (k + 1) * LEAF] = jnp.where(keep, v.astype(F32), 0.0).astype(BF16)
        u_out[b] = jnp.concatenate([u_ref[b, 0], u_ref[b, 1]], axis=0).T
        return carry

    lax.fori_loop(0, NB, step, 0, unroll=4)


def prepare(rank, far_rows, far_cols, near_rows, near_cols, u, v):
    operands = (rank, far_rows, far_cols, near_rows, near_cols, u, v)
    operands = [pltpu.with_memory_space_constraint(x, pltpu.HBM) for x in operands]
    return pl.pallas_call(
        prepare_kernel,
        out_shape=(
            pltpu.VMEM((NB, LEAF, 2 * RMAX), BF16),
            pltpu.VMEM((NB, RMAX, 2 * LEAF), BF16),
            pltpu.SMEM((COUNTS + 2 * GROUPS,), jnp.int32),
        ),
        in_specs=[ANY] * 7,
        out_specs=(VMEM, VMEM, SMEM),
        scratch_shapes=[
            pltpu.SMEM((NB,), jnp.int32),
            pltpu.SMEM((NB,), jnp.int32),
            pltpu.SMEM((NB,), jnp.int32),
            pltpu.SMEM((NN,), jnp.int32),
            pltpu.SMEM((NN,), jnp.int32),
            pltpu.VMEM((NB, 2, RMAX, LEAF), BF16),
            pltpu.VMEM((NB, 2, RMAX, LEAF), BF16),
            pltpu.SemaphoreType.DMA((7,)),
        ],
        compiler_params=limit(4),
        cost_estimate=cost(8),
    )(*operands)


def cost(mib):
    return pl.CostEstimate(flops=0, bytes_accessed=mib << 20, transcendentals=0)


def load(piece, trial, base):
    for q in range(8):
        x = piece[q * LEAF : (q + 1) * LEAF, :]
        trial[base + q, :LEAF, :] = x
        trial[base + q, LEAF:, :] = swap_parts(x)


def work(group, lists, u_ref, v_ref, near_ref, trial, total):
    def entries(kind, q):
        found = []
        for k in range(WAYS):
            e = lists[(kind * GROUPS + group) * LIST + q * WAYS + k]
            found.append((e & 63, (e >> 6) & 31, e >> 11))
        return found

    def far_step(q, carry):
        found = entries(0, q)
        coeffs = [
            jnp.dot(v_ref[b], trial[slot], preferred_element_type=F32).astype(BF16)
            for b, slot, _ in found
        ]
        for coeff, (b, _, target) in zip(coeffs, found):
            both = jnp.concatenate([coeff, swap_parts(coeff)], axis=0)
            total[target] += jnp.dot(u_ref[b], both, preferred_element_type=F32)
        return carry

    def near_step(q, carry):
        for n, slot, target in entries(1, q):
            block = jnp.concatenate([near_ref[n, 0], near_ref[n, 1]], axis=1)
            total[target] += jnp.dot(block, trial[slot], preferred_element_type=F32)
        return carry

    lax.fori_loop(0, lists[COUNTS + group], far_step, 0)
    lax.fori_loop(0, lists[COUNTS + GROUPS + group], near_step, 0)


TOTAL = pltpu.VMEM((SLAB + 1, LEAF, COLS), F32)


def first_kernel(lists, u_ref, v_ref, near_ref, piece, total, trial):
    total[...] = jnp.zeros_like(total)
    load(piece, trial, 0)
    work(0, lists, u_ref, v_ref, near_ref, trial, total)


def second_kernel(lists, u_ref, v_ref, near_ref, piece, _, total, trial):
    load(piece, trial, 0)
    work(1, lists, u_ref, v_ref, near_ref, trial, total)


def third_kernel(lists, u_ref, v_ref, near_ref, ahead, back, _, total, trial, one_ref, two_ref):
    load(ahead, trial, 0)
    load(back, trial, 8)
    work(2, lists, u_ref, v_ref, near_ref, trial, total)
    for t in range(FIRST):
        one_ref[t * LEAF : (t + 1) * LEAF, :] = total[t].astype(BF16)
    for t in range(SLAB // 2 - FIRST):
        two_ref[t * LEAF : (t + 1) * LEAF, :] = total[FIRST + t].astype(BF16)


def fourth_kernel(lists, u_ref, v_ref, near_ref, trial, _, total):
    work(3, lists, u_ref, v_ref, near_ref, trial, total)


def blocks(common, pieces):
    first, ahead, back, two = pieces
    scratch = [pltpu.VMEM((8, 2 * LEAF, COLS), BF16)]
    total = pl.pallas_call(
        first_kernel,
        out_shape=TOTAL,
        in_specs=[SMEM] + [VMEM] * 4,
        out_specs=VMEM,
        scratch_shapes=scratch,
        compiler_params=limit(6),
        cost_estimate=cost(8),
    )(*common, first)
    total = pl.pallas_call(
        second_kernel,
        out_shape=TOTAL,
        in_specs=[SMEM] + [VMEM] * 5,
        out_specs=VMEM,
        scratch_shapes=scratch,
        input_output_aliases={5: 0},
        compiler_params=limit(6),
        cost_estimate=cost(6),
    )(*common, two, total)
    total, trial, one, other = pl.pallas_call(
        third_kernel,
        out_shape=(
            TOTAL,
            pltpu.VMEM((16, 2 * LEAF, COLS), BF16),
            pltpu.VMEM((FIRST * LEAF, COLS), BF16),
            pltpu.VMEM(((SLAB // 2 - FIRST) * LEAF, COLS), BF16),
        ),
        in_specs=[SMEM] + [VMEM] * 6,
        out_specs=(VMEM, VMEM, VMEM, VMEM),
        input_output_aliases={6: 0},
        compiler_params=limit(6),
        cost_estimate=cost(8),
    )(*common, ahead, back, total)
    total = pl.pallas_call(
        fourth_kernel,
        out_shape=TOTAL,
        in_specs=[SMEM] + [VMEM] * 5,
        out_specs=VMEM,
        input_output_aliases={5: 0},
        compiler_params=limit(6),
        cost_estimate=cost(6),
    )(*common, trial, total)
    return (one, other), total


def gather(mine):
    two, back, ahead = [hop(0, step, mine) for step in (2, -1, 1)]
    first = weave([mine, ahead, back, two])
    two, back, ahead = [hop(1, step, first) for step in (2, -1, 1)]
    return [first, ahead, back, two]


def chip_sum(own, swapped, first, count):
    mine = own[SLAB // 2 + first : SLAB // 2 + first + count].reshape(count * LEAF, COLS)
    theirs, first = (swapped[0], first) if first < FIRST else (swapped[1], first - FIRST)
    return mine + theirs[first * LEAF : (first + count) * LEAF].astype(F32)


def cluster(k):
    return pl.ds(pl.multiple_of(k * LEAF, LEAF), LEAF)


def relay_kernel(own, swapped, close, middle, same_ref, cross_ref):
    core = position()[3]
    for owner, out in ((core, same_ref), (1 - core, cross_ref)):
        for i in range(2):
            place = owner * 2 + i

            total = own[SLAB // 2 + 10 + place] + swapped[cluster(10 - FIRST + place), :].astype(F32)
            total += close[cluster(place), :].astype(F32) + middle[cluster(2 + place), :].astype(F32)
            out[i * LEAF : (i + 1) * LEAF, :] = total.astype(BF16)


def relay(own, swapped, close, middle):
    shape = pltpu.VMEM((2 * LEAF, COLS), BF16)
    return pl.pallas_call(
        relay_kernel,
        out_shape=(shape, shape),
        in_specs=[VMEM] * 4,
        out_specs=(VMEM, VMEM),
        compiler_params=limit(4),
    )(own, swapped, close, middle)


def scatter(swapped, own):
    middle = along_z(2, chip_sum(own, swapped, 0, 6).astype(BF16))
    close = along_z(1, chip_sum(own, swapped, 6, 4).astype(BF16))
    same, cross = relay(own, swapped[1], close, middle)
    far = after(middle[: 2 * LEAF], same)
    same, cross = along_z(1, same), along_z(1, cross, 1)
    far = along_z(2, far)
    total = chip_sum(own, swapped, 14, 2) + far.astype(F32)
    return (total + same.astype(F32) + cross.astype(F32)).astype(BF16)


def body(
    incident, perm, far_u, far_v, far_rank, far_rows, far_cols, near_block, near_rows, near_cols
):
    mine = order(perm, incident)
    u, v, lists = prepare(
        far_rank,
        far_rows,
        far_cols,
        near_rows,
        near_cols,
        jnp.swapaxes(far_u, 2, 3),
        jnp.swapaxes(far_v, 2, 3),
    )
    pieces = gather(mine)
    other, own = blocks((lists, u, v, near_block), pieces)
    return scatter([other_core(part) for part in other], own)


def solution(mesh):
    placed = (
        P(("col", "row"), None),
        P(("col", "row"), None),
        P(("row", "col"), None, None, None),
        P(("row", "col"), None, None, None),
        P(("row", "col")),
        P(("row", "col")),
        P(("row", "col")),
        P(("row", "col"), None, None, None),
        P(("row", "col")),
        P(("row", "col")),
    )
    return jax.shard_map(
        body, mesh=mesh, in_specs=placed, out_specs=P(("row", "col"), None), check_vma=False
    )
```

```python
import jax
import jax.numpy as jnp
from jax import lax
from jax.experimental import pallas as pl
from jax.experimental.pallas import tpu as pltpu
from jax.sharding import PartitionSpec as P

LEAF = 128
COLS = 256
HALF = 128
RMAX = 64
NB = 32
NN = 28
NX = 4
NY = 4
NZ = 8
NCORE = 2
SLAB = 32
WAYS = 4
GROUPS = 4
LIST = 36
COUNTS = 2 * GROUPS * LIST
FIRST = 6
F32 = jnp.float32
BF16 = jnp.bfloat16
VMEM = pl.BlockSpec(memory_space=pltpu.VMEM)
SMEM = pl.BlockSpec(memory_space=pltpu.SMEM)
ANY = pl.BlockSpec(memory_space=pl.ANY)


def limit(mib):
    return pltpu.CompilerParams(vmem_limit_bytes=mib << 20)


def position():
    row, col = lax.axis_index("row"), lax.axis_index("col")
    return row // NY, row % NY, col // NCORE, col % NCORE


def hop(turn, step, value):
    pairs = []
    for d in range(NX * NY * NZ * NCORE):
        row, col = divmod(d, NZ * NCORE)
        x, y = divmod(row, NY)
        if (col + turn) % NCORE == 0:
            x = (x + step) % NX
        else:
            y = (y + step) % NY
        pairs.append((d, (x * NY + y) * NZ * NCORE + col))
    return lax.ppermute(value, ("row", "col"), pairs)


def along_z(step, value, turn=0):
    pairs = []
    for d in range(NZ * NCORE):
        z, c = divmod(d, NCORE)
        z = (z + step * (1 - 2 * c)) % NZ
        pairs.append((d, z * NCORE + (c + turn) % NCORE))
    return lax.ppermute(value, "col", pairs)


def other_core(value):
    return lax.ppermute(value, "col", [(d, d ^ 1) for d in range(NZ * NCORE)])


def after(value, earlier):
    return lax.optimization_barrier((value, earlier))[0]


def swap_parts(values):
    return jnp.concatenate([-values[:, HALF:], values[:, :HALF]], axis=1)


def order_kernel(perm_hbm, x_hbm, out_ref, perm_ref, x_ref, perm_sem, x_sem):
    x_copy = pltpu.make_async_copy(x_hbm, x_ref, x_sem)
    perm_copy = pltpu.make_async_copy(perm_hbm, perm_ref, perm_sem)
    x_copy.start()
    perm_copy.start()
    source = lax.broadcasted_iota(jnp.int32, (LEAF, LEAF), 0)
    perm_copy.wait()
    x_copy.wait()
    for k in range(2):
        rows = slice(k * LEAF, (k + 1) * LEAF)
        chosen = (source == perm_ref[k : k + 1, :]).astype(F32).astype(BF16)
        out_ref[rows, :] = lax.dot_general(
            chosen, x_ref[rows, :], (((0,), (0,)), ((), ())), preferred_element_type=F32
        ).astype(BF16)


def order(perm, incident):
    return pl.pallas_call(
        order_kernel,
        out_shape=pltpu.VMEM((2 * LEAF, COLS), BF16),
        in_specs=[ANY, ANY],
        out_specs=VMEM,
        scratch_shapes=[
            pltpu.VMEM((2, LEAF), jnp.int32),
            pltpu.VMEM((2 * LEAF, COLS), BF16),
            pltpu.SemaphoreType.DMA,
            pltpu.SemaphoreType.DMA,
        ],
    )(perm, incident)


def weave_kernel(*refs):
    for q in range(4):
        refs[4][q * 2 * LEAF : (q + 1) * 2 * LEAF, :] = refs[q][...]


def weave(parts):
    return pl.pallas_call(
        weave_kernel,
        out_shape=pltpu.VMEM((8 * LEAF, COLS), BF16),
        in_specs=[VMEM] * 4,
        out_specs=VMEM,
        compiler_params=limit(4),
    )(*parts)


def prepare_kernel(
    rank_hbm,
    far_rows_hbm,
    far_cols_hbm,
    near_rows_hbm,
    near_cols_hbm,
    u_hbm,
    v_hbm,
    u_out,
    v_out,
    lists,
    rank,
    far_rows,
    far_cols,
    near_rows,
    near_cols,
    u_ref,
    v_ref,
    sems,
):
    pairs = (
        (far_rows_hbm, far_rows),
        (far_cols_hbm, far_cols),
        (near_rows_hbm, near_rows),
        (near_cols_hbm, near_cols),
        (rank_hbm, rank),
        (v_hbm, v_ref),
        (u_hbm, u_ref),
    )
    copies = [pltpu.make_async_copy(a, b, sems.at[k]) for k, (a, b) in enumerate(pairs)]
    for copy in copies:
        copy.start()
    my_x, my_y, my_z, my_core = position()

    def gray(d):
        return d ^ (d >> 1)

    def entry(b, row, col):
        k = col & (SLAB - 1)
        r = k >> 1
        dx = gray((my_x - (r >> 2)) & 3)
        dy = gray((my_y - (r & 3)) & 3)
        piece = jnp.where(my_core == 0, dy, dx)
        place = jnp.where(my_core == 0, dx, dy) * 2 + (k & 1)
        i, owner = row & 1, (row >> 1) & 1
        dz = (((row & (SLAB - 1)) >> 2) - my_z) & 7
        straight = (dz & 3) == 0
        handler = jnp.where(straight, owner, dz >> 2)
        steps = jnp.where(handler == 0, dz, 8 - dz)
        near = jnp.where(straight, 14 - 14 * (dz >> 2) + i, 14 - 4 * steps + owner * 2 + i)
        own = jnp.where(handler == my_core, 1, 0)
        target = own * 16 + near
        late = (piece == 1) | (piece == 2)
        group = jnp.where(late, 2 + own, jnp.where(piece == 0, 0, 1))
        slot = jnp.where(piece == 2, 8 + place, place)
        return group, b | (slot << 6) | (target << 11)

    def fill(count, rows, cols, kind):
        for g in range(GROUPS):
            lists[COUNTS + kind * GROUPS + g] = 0

        def step(b, carry):
            group, value = entry(b, rows[b], cols[b])
            at = COUNTS + kind * GROUPS + group
            used = lists[at]
            lists[(kind * GROUPS + group) * LIST + used] = value
            lists[at] = used + 1
            return carry

        lax.fori_loop(0, count, step, 0)

    def blank(k, carry):
        lists[k] = SLAB << 11
        return carry

    lax.fori_loop(0, COUNTS, blank, 0, unroll=8)
    for copy in copies[:4]:
        copy.wait()
    fill(NB, far_rows, far_cols, 0)
    fill(NN, near_rows, near_cols, 1)
    for g in range(GROUPS):
        used = jnp.maximum(lists[COUNTS + g], lists[COUNTS + GROUPS + g])
        lists[COUNTS + g] = (used + WAYS - 1) // WAYS
    for copy in copies[4:]:
        copy.wait()
    line = lax.broadcasted_iota(jnp.int32, (RMAX, LEAF), 0)

    def step(b, carry):
        keep = line < rank[b]
        for k in range(2):
            v = v_ref[b, k]
            v_out[b, :, k * LEAF : (k + 1) * LEAF] = jnp.where(keep, v.astype(F32), 0.0).astype(BF16)
        u_out[b] = jnp.concatenate([u_ref[b, 0], u_ref[b, 1]], axis=0).T
        return carry

    lax.fori_loop(0, NB, step, 0, unroll=4)


def prepare(rank, far_rows, far_cols, near_rows, near_cols, u, v):
    operands = (rank, far_rows, far_cols, near_rows, near_cols, u, v)
    operands = [pltpu.with_memory_space_constraint(x, pltpu.HBM) for x in operands]
    return pl.pallas_call(
        prepare_kernel,
        out_shape=(
            pltpu.VMEM((NB, LEAF, 2 * RMAX), BF16),
            pltpu.VMEM((NB, RMAX, 2 * LEAF), BF16),
            pltpu.SMEM((COUNTS + 2 * GROUPS,), jnp.int32),
        ),
        in_specs=[ANY] * 7,
        out_specs=(VMEM, VMEM, SMEM),
        scratch_shapes=[
            pltpu.SMEM((NB,), jnp.int32),
            pltpu.SMEM((NB,), jnp.int32),
            pltpu.SMEM((NB,), jnp.int32),
            pltpu.SMEM((NN,), jnp.int32),
            pltpu.SMEM((NN,), jnp.int32),
            pltpu.VMEM((NB, 2, RMAX, LEAF), BF16),
            pltpu.VMEM((NB, 2, RMAX, LEAF), BF16),
            pltpu.SemaphoreType.DMA((7,)),
        ],
        compiler_params=limit(4),
        cost_estimate=cost(8),
    )(*operands)


def cost(mib):
    return pl.CostEstimate(flops=0, bytes_accessed=mib << 20, transcendentals=0)


def load(piece, trial, base):
    for q in range(8):
        x = piece[q * LEAF : (q + 1) * LEAF, :]
        trial[base + q, :LEAF, :] = x
        trial[base + q, LEAF:, :] = swap_parts(x)


def work(group, lists, u_ref, v_ref, near_ref, trial, total):
    def entries(kind, q):
        found = []
        for k in range(WAYS):
            e = lists[(kind * GROUPS + group) * LIST + q * WAYS + k]
            found.append((e & 63, (e >> 6) & 31, e >> 11))
        return found

    def step(q, carry):
        far, near = entries(0, q), entries(1, q)
        coeffs = [
            jnp.dot(v_ref[b], trial[slot], preferred_element_type=F32).astype(BF16)
            for b, slot, _ in far
        ]
        terms = []
        for n, slot, _ in near:
            block = jnp.concatenate([near_ref[n, 0], near_ref[n, 1]], axis=1)
            terms.append(jnp.dot(block, trial[slot], preferred_element_type=F32))
        for term, (_, _, target) in zip(terms, near):
            total[target] += term
        for coeff, (b, _, target) in zip(coeffs, far):
            both = jnp.concatenate([coeff, swap_parts(coeff)], axis=0)
            total[target] += jnp.dot(u_ref[b], both, preferred_element_type=F32)
        return carry

    lax.fori_loop(0, lists[COUNTS + group], step, 0)


TOTAL = pltpu.VMEM((SLAB + 1, LEAF, COLS), F32)


def first_kernel(lists, u_ref, v_ref, near_ref, piece, total, trial):
    total[...] = jnp.zeros_like(total)
    load(piece, trial, 0)
    work(0, lists, u_ref, v_ref, near_ref, trial, total)


def second_kernel(lists, u_ref, v_ref, near_ref, piece, _, total, trial):
    load(piece, trial, 0)
    work(1, lists, u_ref, v_ref, near_ref, trial, total)


def third_kernel(lists, u_ref, v_ref, near_ref, ahead, back, _, total, trial, one_ref, two_ref):
    load(ahead, trial, 0)
    load(back, trial, 8)
    work(2, lists, u_ref, v_ref, near_ref, trial, total)
    for t in range(FIRST):
        one_ref[t * LEAF : (t + 1) * LEAF, :] = total[t].astype(BF16)
    for t in range(SLAB // 2 - FIRST):
        two_ref[t * LEAF : (t + 1) * LEAF, :] = total[FIRST + t].astype(BF16)


def fourth_kernel(lists, u_ref, v_ref, near_ref, trial, _, total):
    work(3, lists, u_ref, v_ref, near_ref, trial, total)


def blocks(common, pieces):
    first, ahead, back, two = pieces
    scratch = [pltpu.VMEM((8, 2 * LEAF, COLS), BF16)]
    total = pl.pallas_call(
        first_kernel,
        out_shape=TOTAL,
        in_specs=[SMEM] + [VMEM] * 4,
        out_specs=VMEM,
        scratch_shapes=scratch,
        compiler_params=limit(6),
        cost_estimate=cost(8),
    )(*common, first)
    total = pl.pallas_call(
        second_kernel,
        out_shape=TOTAL,
        in_specs=[SMEM] + [VMEM] * 5,
        out_specs=VMEM,
        scratch_shapes=scratch,
        input_output_aliases={5: 0},
        compiler_params=limit(6),
        cost_estimate=cost(6),
    )(*common, two, total)
    total, trial, one, other = pl.pallas_call(
        third_kernel,
        out_shape=(
            TOTAL,
            pltpu.VMEM((16, 2 * LEAF, COLS), BF16),
            pltpu.VMEM((FIRST * LEAF, COLS), BF16),
            pltpu.VMEM(((SLAB // 2 - FIRST) * LEAF, COLS), BF16),
        ),
        in_specs=[SMEM] + [VMEM] * 6,
        out_specs=(VMEM, VMEM, VMEM, VMEM),
        input_output_aliases={6: 0},
        compiler_params=limit(6),
        cost_estimate=cost(8),
    )(*common, ahead, back, total)
    total = pl.pallas_call(
        fourth_kernel,
        out_shape=TOTAL,
        in_specs=[SMEM] + [VMEM] * 5,
        out_specs=VMEM,
        input_output_aliases={5: 0},
        compiler_params=limit(6),
        cost_estimate=cost(6),
    )(*common, trial, total)
    return (one, other), total


def gather(mine):
    two, back, ahead = [hop(0, step, mine) for step in (2, -1, 1)]
    first = weave([mine, ahead, back, two])
    two, back, ahead = [hop(1, step, first) for step in (2, -1, 1)]
    return [first, ahead, back, two]


def chip_sum(own, swapped, first, count):
    mine = own[SLAB // 2 + first : SLAB // 2 + first + count].reshape(count * LEAF, COLS)
    theirs, first = (swapped[0], first) if first < FIRST else (swapped[1], first - FIRST)
    return mine + theirs[first * LEAF : (first + count) * LEAF].astype(F32)


def cluster(k):
    return pl.ds(pl.multiple_of(k * LEAF, LEAF), LEAF)


def relay_kernel(own, swapped, close, middle, same_ref, cross_ref):
    core = position()[3]
    for owner, out in ((core, same_ref), (1 - core, cross_ref)):
        for i in range(2):
            place = owner * 2 + i

            total = own[SLAB // 2 + 10 + place] + swapped[cluster(10 - FIRST + place), :].astype(F32)
            total += close[cluster(place), :].astype(F32) + middle[cluster(2 + place), :].astype(F32)
            out[i * LEAF : (i + 1) * LEAF, :] = total.astype(BF16)


def relay(own, swapped, close, middle):
    shape = pltpu.VMEM((2 * LEAF, COLS), BF16)
    return pl.pallas_call(
        relay_kernel,
        out_shape=(shape, shape),
        in_specs=[VMEM] * 4,
        out_specs=(VMEM, VMEM),
        compiler_params=limit(4),
    )(own, swapped, close, middle)


def scatter(swapped, own):
    middle = along_z(2, chip_sum(own, swapped, 0, 6).astype(BF16))
    close = along_z(1, chip_sum(own, swapped, 6, 4).astype(BF16))
    same, cross = relay(own, swapped[1], close, middle)
    far = after(middle[: 2 * LEAF], same)
    same, cross = along_z(1, same), along_z(1, cross, 1)
    far = along_z(2, far)
    total = chip_sum(own, swapped, 14, 2) + far.astype(F32)
    return (total + same.astype(F32) + cross.astype(F32)).astype(BF16)


def body(
    incident, perm, far_u, far_v, far_rank, far_rows, far_cols, near_block, near_rows, near_cols
):
    mine = order(perm, incident)
    u, v, lists = prepare(
        far_rank,
        far_rows,
        far_cols,
        near_rows,
        near_cols,
        jnp.swapaxes(far_u, 2, 3),
        jnp.swapaxes(far_v, 2, 3),
    )
    pieces = gather(mine)
    other, own = blocks((lists, u, v, near_block), pieces)
    return scatter([other_core(part) for part in other], own)


def solution(mesh):
    placed = (
        P(("col", "row"), None),
        P(("col", "row"), None),
        P(("row", "col"), None, None, None),
        P(("row", "col"), None, None, None),
        P(("row", "col")),
        P(("row", "col")),
        P(("row", "col")),
        P(("row", "col"), None, None, None),
        P(("row", "col")),
        P(("row", "col")),
    )
    return jax.shard_map(
        body, mesh=mesh, in_specs=placed, out_specs=P(("row", "col"), None), check_vma=False
    )
```

```python
import jax
import jax.numpy as jnp
from jax import lax
from jax.experimental import pallas as pl
from jax.experimental.pallas import tpu as pltpu
from jax.sharding import PartitionSpec as P

LEAF = 128
COLS = 256
HALF = 128
RMAX = 64
NB = 32
NN = 28
NX = 4
NY = 4
NZ = 8
NCORE = 2
SLAB = 32
WAYS = 6
GROUPS = 4
LIST = 36
COUNTS = 2 * GROUPS * LIST
FIRST = 6
F32 = jnp.float32
BF16 = jnp.bfloat16
VMEM = pl.BlockSpec(memory_space=pltpu.VMEM)
SMEM = pl.BlockSpec(memory_space=pltpu.SMEM)
ANY = pl.BlockSpec(memory_space=pl.ANY)


def limit(mib):
    return pltpu.CompilerParams(vmem_limit_bytes=mib << 20)


def position():
    row, col = lax.axis_index("row"), lax.axis_index("col")
    return row // NY, row % NY, col // NCORE, col % NCORE


def hop(turn, step, value):
    pairs = []
    for d in range(NX * NY * NZ * NCORE):
        row, col = divmod(d, NZ * NCORE)
        x, y = divmod(row, NY)
        if (col + turn) % NCORE == 0:
            x = (x + step) % NX
        else:
            y = (y + step) % NY
        pairs.append((d, (x * NY + y) * NZ * NCORE + col))
    return lax.ppermute(value, ("row", "col"), pairs)


def along_z(step, value, turn=0):
    pairs = []
    for d in range(NZ * NCORE):
        z, c = divmod(d, NCORE)
        z = (z + step * (1 - 2 * c)) % NZ
        pairs.append((d, z * NCORE + (c + turn) % NCORE))
    return lax.ppermute(value, "col", pairs)


def other_core(value):
    return lax.ppermute(value, "col", [(d, d ^ 1) for d in range(NZ * NCORE)])


def after(value, earlier):
    return lax.optimization_barrier((value, earlier))[0]


def swap_parts(values):
    return jnp.concatenate([-values[:, HALF:], values[:, :HALF]], axis=1)


def order_kernel(perm_hbm, x_hbm, out_ref, perm_ref, x_ref, perm_sem, x_sem):
    x_copy = pltpu.make_async_copy(x_hbm, x_ref, x_sem)
    perm_copy = pltpu.make_async_copy(perm_hbm, perm_ref, perm_sem)
    x_copy.start()
    perm_copy.start()
    source = lax.broadcasted_iota(jnp.int32, (LEAF, LEAF), 0)
    perm_copy.wait()
    x_copy.wait()
    for k in range(2):
        rows = slice(k * LEAF, (k + 1) * LEAF)
        chosen = (source == perm_ref[k : k + 1, :]).astype(F32).astype(BF16)
        out_ref[rows, :] = lax.dot_general(
            chosen, x_ref[rows, :], (((0,), (0,)), ((), ())), preferred_element_type=F32
        ).astype(BF16)


def order(perm, incident):
    return pl.pallas_call(
        order_kernel,
        out_shape=pltpu.VMEM((2 * LEAF, COLS), BF16),
        in_specs=[ANY, ANY],
        out_specs=VMEM,
        scratch_shapes=[
            pltpu.VMEM((2, LEAF), jnp.int32),
            pltpu.VMEM((2 * LEAF, COLS), BF16),
            pltpu.SemaphoreType.DMA,
            pltpu.SemaphoreType.DMA,
        ],
    )(perm, incident)


def weave_kernel(*refs):
    for q in range(4):
        refs[4][q * 2 * LEAF : (q + 1) * 2 * LEAF, :] = refs[q][...]


def weave(parts):
    return pl.pallas_call(
        weave_kernel,
        out_shape=pltpu.VMEM((8 * LEAF, COLS), BF16),
        in_specs=[VMEM] * 4,
        out_specs=VMEM,
        compiler_params=limit(4),
    )(*parts)


def prepare_kernel(
    rank_hbm,
    far_rows_hbm,
    far_cols_hbm,
    near_rows_hbm,
    near_cols_hbm,
    u_hbm,
    v_hbm,
    u_out,
    v_out,
    lists,
    rank,
    far_rows,
    far_cols,
    near_rows,
    near_cols,
    u_ref,
    v_ref,
    sems,
):
    pairs = (
        (far_rows_hbm, far_rows),
        (far_cols_hbm, far_cols),
        (near_rows_hbm, near_rows),
        (near_cols_hbm, near_cols),
        (rank_hbm, rank),
        (v_hbm, v_ref),
        (u_hbm, u_ref),
    )
    copies = [pltpu.make_async_copy(a, b, sems.at[k]) for k, (a, b) in enumerate(pairs)]
    for copy in copies:
        copy.start()
    my_x, my_y, my_z, my_core = position()

    def gray(d):
        return d ^ (d >> 1)

    def entry(b, row, col):
        k = col & (SLAB - 1)
        r = k >> 1
        dx = gray((my_x - (r >> 2)) & 3)
        dy = gray((my_y - (r & 3)) & 3)
        piece = jnp.where(my_core == 0, dy, dx)
        place = jnp.where(my_core == 0, dx, dy) * 2 + (k & 1)
        i, owner = row & 1, (row >> 1) & 1
        dz = (((row & (SLAB - 1)) >> 2) - my_z) & 7
        straight = (dz & 3) == 0
        handler = jnp.where(straight, owner, dz >> 2)
        steps = jnp.where(handler == 0, dz, 8 - dz)
        near = jnp.where(straight, 14 - 14 * (dz >> 2) + i, 14 - 4 * steps + owner * 2 + i)
        own = jnp.where(handler == my_core, 1, 0)
        target = own * 16 + near
        late = (piece == 1) | (piece == 2)
        group = jnp.where(late, 2 + own, jnp.where(piece == 0, 0, 1))
        slot = jnp.where(piece == 2, 8 + place, place)
        return group, b | (slot << 6) | (target << 11)

    def fill(count, rows, cols, kind):
        for g in range(GROUPS):
            lists[COUNTS + kind * GROUPS + g] = 0

        def step(b, carry):
            group, value = entry(b, rows[b], cols[b])
            at = COUNTS + kind * GROUPS + group
            used = lists[at]
            lists[(kind * GROUPS + group) * LIST + used] = value
            lists[at] = used + 1
            return carry

        lax.fori_loop(0, count, step, 0)

    def blank(k, carry):
        lists[k] = SLAB << 11
        return carry

    lax.fori_loop(0, COUNTS, blank, 0, unroll=8)
    for copy in copies[:4]:
        copy.wait()
    fill(NB, far_rows, far_cols, 0)
    fill(NN, near_rows, near_cols, 1)
    for g in range(GROUPS):
        used = jnp.maximum(lists[COUNTS + g], lists[COUNTS + GROUPS + g])
        lists[COUNTS + g] = (used + WAYS - 1) // WAYS
    for copy in copies[4:]:
        copy.wait()
    line = lax.broadcasted_iota(jnp.int32, (RMAX, LEAF), 0)

    def step(b, carry):
        keep = line < rank[b]
        for k in range(2):
            v = v_ref[b, k]
            v_out[b, :, k * LEAF : (k + 1) * LEAF] = jnp.where(keep, v.astype(F32), 0.0).astype(BF16)
        u_out[b] = jnp.concatenate([u_ref[b, 0], u_ref[b, 1]], axis=0).T
        return carry

    lax.fori_loop(0, NB, step, 0, unroll=4)


def prepare(rank, far_rows, far_cols, near_rows, near_cols, u, v):
    operands = (rank, far_rows, far_cols, near_rows, near_cols, u, v)
    operands = [pltpu.with_memory_space_constraint(x, pltpu.HBM) for x in operands]
    return pl.pallas_call(
        prepare_kernel,
        out_shape=(
            pltpu.VMEM((NB, LEAF, 2 * RMAX), BF16),
            pltpu.VMEM((NB, RMAX, 2 * LEAF), BF16),
            pltpu.SMEM((COUNTS + 2 * GROUPS,), jnp.int32),
        ),
        in_specs=[ANY] * 7,
        out_specs=(VMEM, VMEM, SMEM),
        scratch_shapes=[
            pltpu.SMEM((NB,), jnp.int32),
            pltpu.SMEM((NB,), jnp.int32),
            pltpu.SMEM((NB,), jnp.int32),
            pltpu.SMEM((NN,), jnp.int32),
            pltpu.SMEM((NN,), jnp.int32),
            pltpu.VMEM((NB, 2, RMAX, LEAF), BF16),
            pltpu.VMEM((NB, 2, RMAX, LEAF), BF16),
            pltpu.SemaphoreType.DMA((7,)),
        ],
        compiler_params=limit(4),
        cost_estimate=cost(8),
    )(*operands)


def cost(mib):
    return pl.CostEstimate(flops=0, bytes_accessed=mib << 20, transcendentals=0)


def load(piece, trial, base):
    for q in range(8):
        x = piece[q * LEAF : (q + 1) * LEAF, :]
        trial[base + q, :LEAF, :] = x
        trial[base + q, LEAF:, :] = swap_parts(x)


def work(group, lists, u_ref, v_ref, near_ref, trial, total):
    def entries(kind, q):
        found = []
        for k in range(WAYS):
            e = lists[(kind * GROUPS + group) * LIST + q * WAYS + k]
            found.append((e & 63, (e >> 6) & 31, e >> 11))
        return found

    def step(q, carry):
        far, near = entries(0, q), entries(1, q)
        coeffs = [
            jnp.dot(v_ref[b], trial[slot], preferred_element_type=F32).astype(BF16)
            for b, slot, _ in far
        ]
        terms = []
        for n, slot, _ in near:
            block = jnp.concatenate([near_ref[n, 0], near_ref[n, 1]], axis=1)
            terms.append(jnp.dot(block, trial[slot], preferred_element_type=F32))
        for term, (_, _, target) in zip(terms, near):
            total[target] += term
        for coeff, (b, _, target) in zip(coeffs, far):
            both = jnp.concatenate([coeff, swap_parts(coeff)], axis=0)
            total[target] += jnp.dot(u_ref[b], both, preferred_element_type=F32)
        return carry

    lax.fori_loop(0, lists[COUNTS + group], step, 0)


TOTAL = pltpu.VMEM((SLAB + 1, LEAF, COLS), F32)


def first_kernel(lists, u_ref, v_ref, near_ref, piece, total, trial):
    total[...] = jnp.zeros_like(total)
    load(piece, trial, 0)
    work(0, lists, u_ref, v_ref, near_ref, trial, total)


def second_kernel(lists, u_ref, v_ref, near_ref, piece, _, total, trial):
    load(piece, trial, 0)
    work(1, lists, u_ref, v_ref, near_ref, trial, total)


def third_kernel(lists, u_ref, v_ref, near_ref, ahead, back, _, total, trial, one_ref, two_ref):
    load(ahead, trial, 0)
    load(back, trial, 8)
    work(2, lists, u_ref, v_ref, near_ref, trial, total)
    for t in range(FIRST):
        one_ref[t * LEAF : (t + 1) * LEAF, :] = total[t].astype(BF16)
    for t in range(SLAB // 2 - FIRST):
        two_ref[t * LEAF : (t + 1) * LEAF, :] = total[FIRST + t].astype(BF16)


def fourth_kernel(lists, u_ref, v_ref, near_ref, trial, _, total):
    work(3, lists, u_ref, v_ref, near_ref, trial, total)


def blocks(common, pieces):
    first, ahead, back, two = pieces
    scratch = [pltpu.VMEM((8, 2 * LEAF, COLS), BF16)]
    total = pl.pallas_call(
        first_kernel,
        out_shape=TOTAL,
        in_specs=[SMEM] + [VMEM] * 4,
        out_specs=VMEM,
        scratch_shapes=scratch,
        compiler_params=limit(6),
        cost_estimate=cost(8),
    )(*common, first)
    total = pl.pallas_call(
        second_kernel,
        out_shape=TOTAL,
        in_specs=[SMEM] + [VMEM] * 5,
        out_specs=VMEM,
        scratch_shapes=scratch,
        input_output_aliases={5: 0},
        compiler_params=limit(6),
        cost_estimate=cost(6),
    )(*common, two, total)
    total, trial, one, other = pl.pallas_call(
        third_kernel,
        out_shape=(
            TOTAL,
            pltpu.VMEM((16, 2 * LEAF, COLS), BF16),
            pltpu.VMEM((FIRST * LEAF, COLS), BF16),
            pltpu.VMEM(((SLAB // 2 - FIRST) * LEAF, COLS), BF16),
        ),
        in_specs=[SMEM] + [VMEM] * 6,
        out_specs=(VMEM, VMEM, VMEM, VMEM),
        input_output_aliases={6: 0},
        compiler_params=limit(6),
        cost_estimate=cost(8),
    )(*common, ahead, back, total)
    total = pl.pallas_call(
        fourth_kernel,
        out_shape=TOTAL,
        in_specs=[SMEM] + [VMEM] * 5,
        out_specs=VMEM,
        input_output_aliases={5: 0},
        compiler_params=limit(6),
        cost_estimate=cost(6),
    )(*common, trial, total)
    return (one, other), total


def gather(mine):
    two, back, ahead = [hop(0, step, mine) for step in (2, -1, 1)]
    first = weave([mine, ahead, back, two])
    two, back, ahead = [hop(1, step, first) for step in (2, -1, 1)]
    return [first, ahead, back, two]


def chip_sum(own, swapped, first, count):
    mine = own[SLAB // 2 + first : SLAB // 2 + first + count].reshape(count * LEAF, COLS)
    theirs, first = (swapped[0], first) if first < FIRST else (swapped[1], first - FIRST)
    return mine + theirs[first * LEAF : (first + count) * LEAF].astype(F32)


def cluster(k):
    return pl.ds(pl.multiple_of(k * LEAF, LEAF), LEAF)


def relay_kernel(own, swapped, close, middle, same_ref, cross_ref):
    core = position()[3]
    for owner, out in ((core, same_ref), (1 - core, cross_ref)):
        for i in range(2):
            place = owner * 2 + i

            total = own[SLAB // 2 + 10 + place] + swapped[cluster(10 - FIRST + place), :].astype(F32)
            total += close[cluster(place), :].astype(F32) + middle[cluster(2 + place), :].astype(F32)
            out[i * LEAF : (i + 1) * LEAF, :] = total.astype(BF16)


def relay(own, swapped, close, middle):
    shape = pltpu.VMEM((2 * LEAF, COLS), BF16)
    return pl.pallas_call(
        relay_kernel,
        out_shape=(shape, shape),
        in_specs=[VMEM] * 4,
        out_specs=(VMEM, VMEM),
        compiler_params=limit(4),
    )(own, swapped, close, middle)


def scatter(swapped, own):
    middle = along_z(2, chip_sum(own, swapped, 0, 6).astype(BF16))
    close = along_z(1, chip_sum(own, swapped, 6, 4).astype(BF16))
    same, cross = relay(own, swapped[1], close, middle)
    far = after(middle[: 2 * LEAF], same)
    same, cross = along_z(1, same), along_z(1, cross, 1)
    far = along_z(2, far)
    total = chip_sum(own, swapped, 14, 2) + far.astype(F32)
    return (total + same.astype(F32) + cross.astype(F32)).astype(BF16)


def body(
    incident, perm, far_u, far_v, far_rank, far_rows, far_cols, near_block, near_rows, near_cols
):
    mine = order(perm, incident)
    u, v, lists = prepare(
        far_rank,
        far_rows,
        far_cols,
        near_rows,
        near_cols,
        jnp.swapaxes(far_u, 2, 3),
        jnp.swapaxes(far_v, 2, 3),
    )
    pieces = gather(mine)
    other, own = blocks((lists, u, v, near_block), pieces)
    return scatter([other_core(part) for part in other], own)


def solution(mesh):
    placed = (
        P(("col", "row"), None),
        P(("col", "row"), None),
        P(("row", "col"), None, None, None),
        P(("row", "col"), None, None, None),
        P(("row", "col")),
        P(("row", "col")),
        P(("row", "col")),
        P(("row", "col"), None, None, None),
        P(("row", "col")),
        P(("row", "col")),
    )
    return jax.shard_map(
        body, mesh=mesh, in_specs=placed, out_specs=P(("row", "col"), None), check_vma=False
    )
```

```python
import jax
import jax.numpy as jnp
from jax import lax
from jax.experimental import pallas as pl
from jax.experimental.pallas import tpu as pltpu
from jax.sharding import PartitionSpec as P

LEAF = 128
COLS = 256
HALF = 128
RMAX = 64
NB = 32
NN = 28
NX = 4
NY = 4
NZ = 8
NCORE = 2
SLAB = 32
WAYS = 6
GROUPS = 4
LIST = 36
COUNTS = 2 * GROUPS * LIST
FIRST = 6
F32 = jnp.float32
BF16 = jnp.bfloat16
VMEM = pl.BlockSpec(memory_space=pltpu.VMEM)
SMEM = pl.BlockSpec(memory_space=pltpu.SMEM)
ANY = pl.BlockSpec(memory_space=pl.ANY)


def limit(mib):
    return pltpu.CompilerParams(vmem_limit_bytes=mib << 20)


def position():
    row, col = lax.axis_index("row"), lax.axis_index("col")
    return row // NY, row % NY, col // NCORE, col % NCORE


def hop(turn, step, value):
    pairs = []
    for d in range(NX * NY * NZ * NCORE):
        row, col = divmod(d, NZ * NCORE)
        x, y = divmod(row, NY)
        if (col + turn) % NCORE == 0:
            x = (x + step) % NX
        else:
            y = (y + step) % NY
        pairs.append((d, (x * NY + y) * NZ * NCORE + col))
    return lax.ppermute(value, ("row", "col"), pairs)


def along_z(step, value, turn=0):
    pairs = []
    for d in range(NZ * NCORE):
        z, c = divmod(d, NCORE)
        z = (z + step * (1 - 2 * c)) % NZ
        pairs.append((d, z * NCORE + (c + turn) % NCORE))
    return lax.ppermute(value, "col", pairs)


def other_core(value):
    return lax.ppermute(value, "col", [(d, d ^ 1) for d in range(NZ * NCORE)])


def after(value, earlier):
    return lax.optimization_barrier((value, earlier))[0]


def swap_parts(values):
    return jnp.concatenate([-values[:, HALF:], values[:, :HALF]], axis=1)


def order_kernel(perm_hbm, x_hbm, out_ref, perm_ref, x_ref, perm_sem, x_sem):
    x_copy = pltpu.make_async_copy(x_hbm, x_ref, x_sem)
    perm_copy = pltpu.make_async_copy(perm_hbm, perm_ref, perm_sem)
    x_copy.start()
    perm_copy.start()
    source = lax.broadcasted_iota(jnp.int32, (LEAF, LEAF), 0)
    perm_copy.wait()
    x_copy.wait()
    for k in range(2):
        rows = slice(k * LEAF, (k + 1) * LEAF)
        chosen = (source == perm_ref[k : k + 1, :]).astype(F32).astype(BF16)
        out_ref[rows, :] = lax.dot_general(
            chosen, x_ref[rows, :], (((0,), (0,)), ((), ())), preferred_element_type=F32
        ).astype(BF16)


def order(perm, incident):
    return pl.pallas_call(
        order_kernel,
        out_shape=pltpu.VMEM((2 * LEAF, COLS), BF16),
        in_specs=[ANY, ANY],
        out_specs=VMEM,
        scratch_shapes=[
            pltpu.VMEM((2, LEAF), jnp.int32),
            pltpu.VMEM((2 * LEAF, COLS), BF16),
            pltpu.SemaphoreType.DMA,
            pltpu.SemaphoreType.DMA,
        ],
    )(perm, incident)


def weave_kernel(*refs):
    for q in range(4):
        refs[4][q * 2 * LEAF : (q + 1) * 2 * LEAF, :] = refs[q][...]


def weave(parts):
    return pl.pallas_call(
        weave_kernel,
        out_shape=pltpu.VMEM((8 * LEAF, COLS), BF16),
        in_specs=[VMEM] * 4,
        out_specs=VMEM,
        compiler_params=limit(4),
    )(*parts)


def prepare_kernel(
    rank_hbm,
    far_rows_hbm,
    far_cols_hbm,
    near_rows_hbm,
    near_cols_hbm,
    u_hbm,
    v_hbm,
    u_out,
    v_out,
    lists,
    rank,
    far_rows,
    far_cols,
    near_rows,
    near_cols,
    u_ref,
    v_ref,
    sems,
):
    pairs = (
        (far_rows_hbm, far_rows),
        (far_cols_hbm, far_cols),
        (near_rows_hbm, near_rows),
        (near_cols_hbm, near_cols),
        (rank_hbm, rank),
        (v_hbm, v_ref),
        (u_hbm, u_ref),
    )
    copies = [pltpu.make_async_copy(a, b, sems.at[k]) for k, (a, b) in enumerate(pairs)]
    for copy in copies:
        copy.start()
    my_x, my_y, my_z, my_core = position()

    def gray(d):
        return d ^ (d >> 1)

    def entry(b, row, col):
        k = col & (SLAB - 1)
        r = k >> 1
        dx = gray((my_x - (r >> 2)) & 3)
        dy = gray((my_y - (r & 3)) & 3)
        piece = jnp.where(my_core == 0, dy, dx)
        place = jnp.where(my_core == 0, dx, dy) * 2 + (k & 1)
        i, owner = row & 1, (row >> 1) & 1
        dz = (((row & (SLAB - 1)) >> 2) - my_z) & 7
        straight = (dz & 3) == 0
        handler = jnp.where(straight, owner, dz >> 2)
        steps = jnp.where(handler == 0, dz, 8 - dz)
        near = jnp.where(straight, 14 - 14 * (dz >> 2) + i, 14 - 4 * steps + owner * 2 + i)
        own = jnp.where(handler == my_core, 1, 0)
        target = own * 16 + near
        late = (piece == 2) | (piece == 3)
        group = jnp.where(late, 2 + own, jnp.where(piece == 0, 0, 1))
        slot = jnp.where(piece == 3, 8 + place, place)
        return group, b | (slot << 6) | (target << 11)

    def fill(count, rows, cols, kind):
        for g in range(GROUPS):
            lists[COUNTS + kind * GROUPS + g] = 0

        def step(b, carry):
            group, value = entry(b, rows[b], cols[b])
            at = COUNTS + kind * GROUPS + group
            used = lists[at]
            lists[(kind * GROUPS + group) * LIST + used] = value
            lists[at] = used + 1
            return carry

        lax.fori_loop(0, count, step, 0)

    def blank(k, carry):
        lists[k] = SLAB << 11
        return carry

    lax.fori_loop(0, COUNTS, blank, 0, unroll=8)
    for copy in copies[:4]:
        copy.wait()
    fill(NB, far_rows, far_cols, 0)
    fill(NN, near_rows, near_cols, 1)
    for g in range(GROUPS):
        used = jnp.maximum(lists[COUNTS + g], lists[COUNTS + GROUPS + g])
        lists[COUNTS + g] = (used + WAYS - 1) // WAYS
    for copy in copies[4:]:
        copy.wait()
    line = lax.broadcasted_iota(jnp.int32, (RMAX, LEAF), 0)

    def step(b, carry):
        keep = line < rank[b]
        for k in range(2):
            v = v_ref[b, k]
            v_out[b, :, k * LEAF : (k + 1) * LEAF] = jnp.where(keep, v.astype(F32), 0.0).astype(BF16)
        u_out[b] = jnp.concatenate([u_ref[b, 0], u_ref[b, 1]], axis=0).T
        return carry

    lax.fori_loop(0, NB, step, 0, unroll=4)


def prepare(rank, far_rows, far_cols, near_rows, near_cols, u, v):
    operands = (rank, far_rows, far_cols, near_rows, near_cols, u, v)
    operands = [pltpu.with_memory_space_constraint(x, pltpu.HBM) for x in operands]
    return pl.pallas_call(
        prepare_kernel,
        out_shape=(
            pltpu.VMEM((NB, LEAF, 2 * RMAX), BF16),
            pltpu.VMEM((NB, RMAX, 2 * LEAF), BF16),
            pltpu.SMEM((COUNTS + 2 * GROUPS,), jnp.int32),
        ),
        in_specs=[ANY] * 7,
        out_specs=(VMEM, VMEM, SMEM),
        scratch_shapes=[
            pltpu.SMEM((NB,), jnp.int32),
            pltpu.SMEM((NB,), jnp.int32),
            pltpu.SMEM((NB,), jnp.int32),
            pltpu.SMEM((NN,), jnp.int32),
            pltpu.SMEM((NN,), jnp.int32),
            pltpu.VMEM((NB, 2, RMAX, LEAF), BF16),
            pltpu.VMEM((NB, 2, RMAX, LEAF), BF16),
            pltpu.SemaphoreType.DMA((7,)),
        ],
        compiler_params=limit(4),
        cost_estimate=cost(8),
    )(*operands)


def cost(mib):
    return pl.CostEstimate(flops=0, bytes_accessed=mib << 20, transcendentals=0)


def load(piece, trial, base):
    for q in range(8):
        x = piece[q * LEAF : (q + 1) * LEAF, :]
        trial[base + q, :LEAF, :] = x
        trial[base + q, LEAF:, :] = swap_parts(x)


def work(group, lists, u_ref, v_ref, near_ref, trial, total):
    def entries(kind, q):
        found = []
        for k in range(WAYS):
            e = lists[(kind * GROUPS + group) * LIST + q * WAYS + k]
            found.append((e & 63, (e >> 6) & 31, e >> 11))
        return found

    def step(q, carry):
        far, near = entries(0, q), entries(1, q)
        coeffs = [
            jnp.dot(v_ref[b], trial[slot], preferred_element_type=F32).astype(BF16)
            for b, slot, _ in far
        ]
        terms = []
        for n, slot, _ in near:
            block = jnp.concatenate([near_ref[n, 0], near_ref[n, 1]], axis=1)
            terms.append(jnp.dot(block, trial[slot], preferred_element_type=F32))
        for term, (_, _, target) in zip(terms, near):
            total[target] += term
        for coeff, (b, _, target) in zip(coeffs, far):
            both = jnp.concatenate([coeff, swap_parts(coeff)], axis=0)
            total[target] += jnp.dot(u_ref[b], both, preferred_element_type=F32)
        return carry

    lax.fori_loop(0, lists[COUNTS + group], step, 0)


TOTAL = pltpu.VMEM((SLAB + 1, LEAF, COLS), F32)


def first_kernel(lists, u_ref, v_ref, near_ref, piece, total, trial):
    total[...] = jnp.zeros_like(total)
    load(piece, trial, 0)
    work(0, lists, u_ref, v_ref, near_ref, trial, total)


def second_kernel(lists, u_ref, v_ref, near_ref, piece, _, total, trial):
    load(piece, trial, 0)
    work(1, lists, u_ref, v_ref, near_ref, trial, total)


def third_kernel(lists, u_ref, v_ref, near_ref, back, two, _, total, trial, one_ref, two_ref):
    load(back, trial, 0)
    load(two, trial, 8)
    work(2, lists, u_ref, v_ref, near_ref, trial, total)
    for t in range(FIRST):
        one_ref[t * LEAF : (t + 1) * LEAF, :] = total[t].astype(BF16)
    for t in range(SLAB // 2 - FIRST):
        two_ref[t * LEAF : (t + 1) * LEAF, :] = total[FIRST + t].astype(BF16)


def fourth_kernel(lists, u_ref, v_ref, near_ref, trial, _, total):
    work(3, lists, u_ref, v_ref, near_ref, trial, total)


def blocks(common, pieces):
    first, ahead, back, two = pieces
    scratch = [pltpu.VMEM((8, 2 * LEAF, COLS), BF16)]
    total = pl.pallas_call(
        first_kernel,
        out_shape=TOTAL,
        in_specs=[SMEM] + [VMEM] * 4,
        out_specs=VMEM,
        scratch_shapes=scratch,
        compiler_params=limit(6),
        cost_estimate=cost(8),
    )(*common, first)
    total = pl.pallas_call(
        second_kernel,
        out_shape=TOTAL,
        in_specs=[SMEM] + [VMEM] * 5,
        out_specs=VMEM,
        scratch_shapes=scratch,
        input_output_aliases={5: 0},
        compiler_params=limit(6),
        cost_estimate=cost(6),
    )(*common, ahead, total)
    total, trial, one, other = pl.pallas_call(
        third_kernel,
        out_shape=(
            TOTAL,
            pltpu.VMEM((16, 2 * LEAF, COLS), BF16),
            pltpu.VMEM((FIRST * LEAF, COLS), BF16),
            pltpu.VMEM(((SLAB // 2 - FIRST) * LEAF, COLS), BF16),
        ),
        in_specs=[SMEM] + [VMEM] * 6,
        out_specs=(VMEM, VMEM, VMEM, VMEM),
        input_output_aliases={6: 0},
        compiler_params=limit(6),
        cost_estimate=cost(8),
    )(*common, back, two, total)
    total = pl.pallas_call(
        fourth_kernel,
        out_shape=TOTAL,
        in_specs=[SMEM] + [VMEM] * 5,
        out_specs=VMEM,
        input_output_aliases={5: 0},
        compiler_params=limit(6),
        cost_estimate=cost(6),
    )(*common, trial, total)
    return (one, other), total


def gather(mine):
    ahead, back, two = [hop(0, step, mine) for step in (1, -1, 2)]
    first = weave([mine, ahead, back, two])
    ahead, back, two = [hop(1, step, first) for step in (1, -1, 2)]
    return [first, ahead, back, two]


def chip_sum(own, swapped, first, count):
    mine = own[SLAB // 2 + first : SLAB // 2 + first + count].reshape(count * LEAF, COLS)
    theirs, first = (swapped[0], first) if first < FIRST else (swapped[1], first - FIRST)
    return mine + theirs[first * LEAF : (first + count) * LEAF].astype(F32)


def cluster(k):
    return pl.ds(pl.multiple_of(k * LEAF, LEAF), LEAF)


def relay_kernel(own, swapped, close, middle, same_ref, cross_ref):
    core = position()[3]
    for owner, out in ((core, same_ref), (1 - core, cross_ref)):
        for i in range(2):
            place = owner * 2 + i

            total = own[SLAB // 2 + 10 + place] + swapped[cluster(10 - FIRST + place), :].astype(F32)
            total += close[cluster(place), :].astype(F32) + middle[cluster(2 + place), :].astype(F32)
            out[i * LEAF : (i + 1) * LEAF, :] = total.astype(BF16)


def relay(own, swapped, close, middle):
    shape = pltpu.VMEM((2 * LEAF, COLS), BF16)
    return pl.pallas_call(
        relay_kernel,
        out_shape=(shape, shape),
        in_specs=[VMEM] * 4,
        out_specs=(VMEM, VMEM),
        compiler_params=limit(4),
    )(own, swapped, close, middle)


def scatter(swapped, own):
    middle = along_z(2, chip_sum(own, swapped, 0, 6).astype(BF16))
    close = along_z(1, chip_sum(own, swapped, 6, 4).astype(BF16))
    same, cross = relay(own, swapped[1], close, middle)
    far = after(middle[: 2 * LEAF], same)
    same, cross = along_z(1, same), along_z(1, cross, 1)
    far = along_z(2, far)
    total = chip_sum(own, swapped, 14, 2) + far.astype(F32)
    return (total + same.astype(F32) + cross.astype(F32)).astype(BF16)


def body(
    incident, perm, far_u, far_v, far_rank, far_rows, far_cols, near_block, near_rows, near_cols
):
    mine = order(perm, incident)
    u, v, lists = prepare(
        far_rank,
        far_rows,
        far_cols,
        near_rows,
        near_cols,
        jnp.swapaxes(far_u, 2, 3),
        jnp.swapaxes(far_v, 2, 3),
    )
    pieces = gather(mine)
    other, own = blocks((lists, u, v, near_block), pieces)
    return scatter([other_core(part) for part in other], own)


def solution(mesh):
    placed = (
        P(("col", "row"), None),
        P(("col", "row"), None),
        P(("row", "col"), None, None, None),
        P(("row", "col"), None, None, None),
        P(("row", "col")),
        P(("row", "col")),
        P(("row", "col")),
        P(("row", "col"), None, None, None),
        P(("row", "col")),
        P(("row", "col")),
    )
    return jax.shard_map(
        body, mesh=mesh, in_specs=placed, out_specs=P(("row", "col"), None), check_vma=False
    )
```
